512 devices in a mesh: aa: 32 (over x, y_lo, core), ba: 16 (over z, y_hi).
Axes of the slice: x: 4, y: 8 (y_hi: 2, y_lo: 4; y = y_hi * 4 + y_lo), z: 8, core: 2. Of those that a mesh axis runs over, the one named last changes fastest.
Arguments:
- field: float32 [32, 2048, 2048], P('aa', None, 'ba'), may hold values from -6 to 6
- gains: float32 [2, 2, 2], replicated, may hold values from 0.25 to 4
Outputs:
- coefficients: float32 [32, 2048, 2048], P(None, 'aa', 'ba')
- rebuilt: float32 [32, 2048, 2048], P('aa', None, 'ba')
The draws below stay inside these ranges and needn't reach their ends.
All inputs are finite; a program needn't handle non-finite values.
Results may differ from the reference program's by a relative error of at most 0.00002.
Values sent between devices are 32-bit elements; how exact they have to be, the bound alone decides.
No kernel may reach another device: no remote copies, remote signals or barrier semaphores. Data moves between devices by JAX's collectives and lax.ppermute only.
A program may use at most 64 MiB of HBM per device.

```python
import math
import jax
import jax.numpy as jnp
from jax import lax

NX = 2048
NY = 2048
NZ = 32


def level_of(key, dims, split, low, largest):
    gain = 1.0
    for dim, blocks in split:
        heights = jax.random.uniform(jax.random.fold_in(jax.random.fold_in(key, 6), dim), (blocks,), jnp.float32, low / len(split), largest / len(split))
        gain = gain * jnp.repeat(jnp.exp(heights), dims[dim] // blocks).reshape((-1,) + (1,) * (len(dims) - 1 - dim))
    return gain


def centred(key, shape, spread, most, pieces=(), held_as=jnp.bfloat16):
    drawn = jax.random.normal(key, shape, jnp.float32) * spread
    if len(pieces) > 0:
        drawn = level_of(key, shape, pieces, -0.22, 0.18) * drawn
    return jnp.clip(drawn, min=-most, max=most).astype(held_as)


def setup_inputs(seed: int = 0) -> dict:
    keys = jax.random.split(jax.random.key(seed), 3)
    field = centred(keys[0], (NZ, NY, NX), 1.0, 6.0, ((0, 32), (2, 16)), jnp.float32)
    gains = jnp.clip(jnp.exp(jax.random.uniform(keys[1], (2, 2, 2), jnp.float32, math.log(0.25), math.log(4.0))), 0.25, 4.0)
    return dict(field=field, gains=gains)


predict_first = -1.586134342059924
update_first = -0.052980118572961
predict_second = 0.882911075530934
update_second = 0.443506852043971
balance = 1.230174104914001


def take_range(values, begin, finish, dimension):
    return lax.slice_in_dim(values, begin, finish, 1, dimension)


def mirror(values, dimension):
    extent = values.shape[dimension]
    lower_rim = jnp.flip(take_range(values, 1, 5, dimension), dimension)
    upper_rim = jnp.flip(take_range(values, extent - 5, extent - 1, dimension), dimension)
    return jnp.concatenate([lower_rim, values, upper_rim], dimension)


def split_parity(extended, dimension):
    length = extended.shape[dimension]
    even_part = lax.slice_in_dim(extended, 0, length, 2, dimension)
    odd_part = lax.slice_in_dim(extended, 1, length, 2, dimension)
    return even_part, odd_part


def alternate(low_band, high_band, dimension):
    joined = jnp.stack([low_band, high_band], axis=dimension + 1)
    new_shape = list(low_band.shape)
    new_shape[dimension] = 2 * new_shape[dimension]
    return joined.reshape(new_shape)


def analyse(extended, dimension):
    even_part, odd_part = split_parity(extended, dimension)
    length = even_part.shape[dimension]
    lift_one = take_range(odd_part, 0, length - 1, dimension) + predict_first * (
        take_range(even_part, 0, length - 1, dimension) + take_range(even_part, 1, length, dimension))
    lift_two = take_range(even_part, 1, length - 1, dimension) + update_first * (
        take_range(lift_one, 0, length - 2, dimension) + take_range(lift_one, 1, length - 1, dimension))
    lift_three = take_range(lift_one, 1, length - 2, dimension) + predict_second * (
        take_range(lift_two, 0, length - 3, dimension) + take_range(lift_two, 1, length - 2, dimension))
    lift_four = take_range(lift_two, 1, length - 3, dimension) + update_second * (
        take_range(lift_three, 0, length - 4, dimension) + take_range(lift_three, 1, length - 3, dimension))
    high_band = take_range(lift_three, 1, length - 3, dimension)
    return alternate(lift_four / balance, high_band * balance, dimension)


def synthesise(extended, dimension):
    even_part, odd_part = split_parity(extended, dimension)
    length = even_part.shape[dimension]
    low_band = even_part * balance
    high_band = odd_part / balance
    lift_one = take_range(low_band, 1, length, dimension) - update_second * (
        take_range(high_band, 0, length - 1, dimension) + take_range(high_band, 1, length, dimension))
    lift_two = take_range(high_band, 1, length - 1, dimension) - predict_second * (
        take_range(lift_one, 0, length - 2, dimension) + take_range(lift_one, 1, length - 1, dimension))
    lift_three = take_range(lift_one, 1, length - 2, dimension) - update_first * (
        take_range(lift_two, 0, length - 3, dimension) + take_range(lift_two, 1, length - 2, dimension))
    lift_four = take_range(lift_two, 1, length - 3, dimension) - predict_first * (
        take_range(lift_three, 0, length - 4, dimension) + take_range(lift_three, 1, length - 3, dimension))
    return alternate(take_range(lift_three, 0, length - 4, dimension), lift_four, dimension)


def apply_gains(coefficients, gains):
    depth_cells, column_cells, row_cells = coefficients.shape
    parity = jnp.arange(row_cells) % 2
    gain_table = jnp.where(parity[None, None, :] == 0, gains[:, :, 0:1], gains[:, :, 1:2])
    grouped = coefficients.reshape(depth_cells // 2, 2, column_cells // 2, 2, row_cells)
    return (grouped * gain_table[None, :, None, :, :]).reshape(coefficients.shape)


def reference(field, gains):
    sectioned = analyse(mirror(field, 2), 2)
    sectioned = analyse(mirror(sectioned, 1), 1)
    coefficients = analyse(mirror(sectioned, 0), 0)
    rebuilt = synthesise(mirror(apply_gains(coefficients, gains), 0), 0)
    rebuilt = synthesise(mirror(rebuilt, 1), 1)
    rebuilt = synthesise(mirror(rebuilt, 2), 2)
    return coefficients, rebuilt
```

```python
import functools

import jax
import jax.numpy as jnp
import numpy as np
from jax import lax
from jax.experimental import pallas as pl
from jax.experimental.pallas import tpu as pltpu
from jax.sharding import PartitionSpec as P

PREDICT_FIRST = -1.586134342059924
UPDATE_FIRST = -0.052980118572961
PREDICT_SECOND = 0.882911075530934
UPDATE_SECOND = 0.443506852043971
BALANCE = 1.230174104914001

X = 128
HALF = X // 2
HALO = 8
ROWS = 8
MARGIN = 16
VMEM_LIMIT = 48 * 1024 * 1024


def edge_matrix():
    unit = np.eye(X)
    s, d = unit[0::2], unit[1::2]
    d1 = [d[n] + PREDICT_FIRST * (s[n] + s[n + 1]) for n in range(HALF - 1)]
    s1 = [None] + [s[n] + UPDATE_FIRST * (d1[n - 1] + d1[n]) for n in range(1, HALF - 1)]
    out = np.zeros((HALO, X))
    out[0] = s[0]
    out[1] = d1[0]
    out[2] = s1[1]
    out[3] = d1[1] + PREDICT_SECOND * (s1[1] + s1[2])
    last = HALF - 1
    out[4] = d[last] + PREDICT_FIRST * s[last]
    out[5] = s[last] + UPDATE_FIRST * d1[last - 1]
    out[6] = d1[last - 1] + PREDICT_SECOND * s1[last - 1]
    return out


def analysis_matrix(left_end, right_end):
    unit = np.eye(2 * X)
    cell, halo = unit[:X], unit[X : X + HALO]
    n_all = HALF
    s = {n: cell[2 * n] for n in range(n_all)}
    d = {n: cell[2 * n + 1] for n in range(n_all)}
    s[n_all] = s[n_all - 1] if right_end else halo[0]
    d1 = {n: d[n] + PREDICT_FIRST * (s[n] + s[n + 1]) for n in range(n_all)}
    d1[n_all] = d1[n_all - 2] if right_end else halo[1]
    d1[-1] = d1[0] if left_end else halo[4] + PREDICT_FIRST * s[0]
    s1 = {n: s[n] + UPDATE_FIRST * (d1[n - 1] + d1[n]) for n in range(n_all + 1)}
    s1[n_all + 1] = s1[n_all - 2] if right_end else halo[2]
    s1[-1] = s1[1] if left_end else halo[5] + UPDATE_FIRST * d1[-1]
    d2 = {n: d1[n] + PREDICT_SECOND * (s1[n] + s1[n + 1]) for n in range(-1, n_all + 1)}
    d2[n_all + 1] = d2[n_all - 3] if right_end else halo[3]
    d2[-2] = d2[1] if left_end else halo[6] + PREDICT_SECOND * s1[-1]
    s2 = {n: s1[n] + UPDATE_SECOND * (d2[n - 1] + d2[n]) for n in range(-1, n_all + 2)}
    out = np.zeros((2 * X, 2 * X))
    for n in range(n_all):
        out[:, 2 * n] = s2[n] / BALANCE
        out[:, 2 * n + 1] = d2[n] * BALANCE
    beyond = [
        s2[n_all] / BALANCE, d2[n_all] * BALANCE, s2[n_all + 1] / BALANCE, d2[n_all + 1] * BALANCE,
        d2[-1] * BALANCE, s2[-1] / BALANCE, d2[-2] * BALANCE,
    ]
    for k, row in enumerate(beyond):
        out[:, X + k] = row
    return out


def synthesis_matrix():
    unit = np.eye(2 * X)
    n_all = HALF
    place = {k: k for k in range(X)}
    place.update({X + k: X + k for k in range(4)})
    place.update({-1: X + 4, -2: X + 5, -3: X + 6})
    s2 = {n: unit[place[2 * n]] * BALANCE for n in range(-1, n_all + 2)}
    d2 = {n: unit[place[2 * n + 1]] / BALANCE for n in range(-2, n_all + 2)}
    s1 = {n: s2[n] - UPDATE_SECOND * (d2[n - 1] + d2[n]) for n in range(-1, n_all + 2)}
    d1 = {n: d2[n] - PREDICT_SECOND * (s1[n] + s1[n + 1]) for n in range(-1, n_all + 1)}
    s = {n: s1[n] - UPDATE_FIRST * (d1[n - 1] + d1[n]) for n in range(n_all + 1)}
    d = {n: d1[n] - PREDICT_FIRST * (s[n] + s[n + 1]) for n in range(n_all)}
    out = np.zeros((2 * X, X))
    for n in range(n_all):
        out[:, 2 * n] = s[n]
        out[:, 2 * n + 1] = d[n]
    return out


def whole(shape):
    return pl.BlockSpec(memory_space=pltpu.VMEM)


def call(kernel, out_shape, n_in, scratch=(), name=None, smem=()):
    return pl.pallas_call(
        kernel,
        out_shape=out_shape,
        in_specs=[
            pl.BlockSpec(memory_space=pltpu.SMEM if i in smem else pltpu.VMEM) for i in range(n_in)
        ],
        out_specs=jax.tree.map(lambda _: pl.BlockSpec(memory_space=pltpu.VMEM), out_shape),
        scratch_shapes=list(scratch),
        compiler_params=pltpu.CompilerParams(vmem_limit_bytes=VMEM_LIMIT),
        name=name,
    )


def fill_line(source, line, ny):
    def body(k, carry):
        at = pl.multiple_of(k * 256, 256)
        line[pl.ds(MARGIN + at, 256), :] = source[pl.ds(at, 256), :]
        return carry

    lax.fori_loop(0, ny // 256, body, 0)
    for k in range(1, 9):
        line[pl.ds(MARGIN - k, 1), :] = line[pl.ds(MARGIN + k, 1), :]
        line[pl.ds(MARGIN + ny - 1 + k, 1), :] = line[pl.ds(MARGIN + ny - 1 - k, 1), :]


def after(rows):
    return pltpu.roll(rows, rows.shape[0] - 1, 0)


def before(rows):
    return pltpu.roll(rows, 1, 0)


def lift_rows(line, target, ny, forward):
    cells = 128
    pairs = cells // 2
    wide = pairs + 8

    def body(k, carry):
        at = pl.multiple_of(k * cells, cells)
        s = line[pl.ds(MARGIN + at - 8, wide, stride=2), :]
        d = line[pl.ds(MARGIN + at - 7, wide, stride=2), :]
        if forward:
            d = d + PREDICT_FIRST * (s + after(s))
            s = s + UPDATE_FIRST * (before(d) + d)
            d = d + PREDICT_SECOND * (s + after(s))
            s = s + UPDATE_SECOND * (before(d) + d)
            s = s * (1.0 / BALANCE)
            d = d * BALANCE
        else:
            s = s * BALANCE
            d = d * (1.0 / BALANCE)
            s = s - UPDATE_SECOND * (before(d) + d)
            d = d - PREDICT_SECOND * (s + after(s))
            s = s - UPDATE_FIRST * (before(d) + d)
            d = d - PREDICT_FIRST * (s + after(s))
        target[pl.ds(at, pairs, stride=2), :] = s[4 : 4 + pairs]
        target[pl.ds(at + 1, pairs, stride=2), :] = d[4 : 4 + pairs]
        return carry

    lax.fori_loop(0, ny // cells, body, 0, unroll=2)


def column_kernel(forward, source, target, line):
    ny = source.shape[0]
    fill_line(source, line, ny)
    lift_rows(line, target, ny, forward)


def columns(values, forward):
    ny = values.shape[0]
    return call(
        functools.partial(column_kernel, forward),
        jax.ShapeDtypeStruct((ny, X), jnp.float32),
        1,
        [pltpu.VMEM((ny + 2 * MARGIN, X), jnp.float32)],
        "analyse_y" if forward else "synthesise_y",
    )(values)


def edge_kernel(values, weights, to_left, to_right):
    edges = lax.dot_general(
        weights[...], values[...], (((1,), (1,)), ((), ())),
        precision=lax.Precision.HIGHEST, preferred_element_type=jnp.float32,
    )
    to_left[...] = edges[0:4]
    to_right[...] = edges[4:8]


def edges_of(values, weights):
    cells = values.shape[0]
    half = jax.ShapeDtypeStruct((4, cells), jnp.float32)
    return call(edge_kernel, (half, half), 2, name="edges_x")(values, weights)


def lift_depth(cells, gain_low, gain_high):
    n = len(cells) // 2
    s, d = cells[0::2], cells[1::2]

    def right(list_, k):
        return list_[k + 1] if k + 1 < n else list_[n - 1]

    def left(list_, k):
        return list_[k - 1] if k > 0 else list_[0]

    d = [d[k] + PREDICT_FIRST * (s[k] + right(s, k)) for k in range(n)]
    s = [s[k] + UPDATE_FIRST * (left(d, k) + d[k]) for k in range(n)]
    d = [d[k] + PREDICT_SECOND * (s[k] + right(s, k)) for k in range(n)]
    s = [s[k] + UPDATE_SECOND * (left(d, k) + d[k]) for k in range(n)]
    low = [v * (1.0 / BALANCE) for v in s]
    high = [v * BALANCE for v in d]
    s = [v * gain_low for v in s]
    d = [v * gain_high for v in d]
    s = [s[k] - UPDATE_SECOND * (left(d, k) + d[k]) for k in range(n)]
    d = [d[k] - PREDICT_SECOND * (s[k] + right(s, k)) for k in range(n)]
    s = [s[k] - UPDATE_FIRST * (left(d, k) + d[k]) for k in range(n)]
    d = [d[k] - PREDICT_FIRST * (s[k] + right(s, k)) for k in range(n)]
    coefficients = [v for pair in zip(low, high) for v in pair]
    rebuilt = [v for pair in zip(s, d) for v in pair]
    return coefficients, rebuilt


def gain_tables(gains, x_odd):
    y_odd = lax.broadcasted_iota(jnp.int32, (ROWS, X), 0) % 2 == 1
    tables = []
    for z in range(2):
        low = jnp.where(x_odd, gains[4 * z + 1], gains[4 * z])
        high = jnp.where(x_odd, gains[4 * z + 3], gains[4 * z + 2])
        tables.append(jnp.where(y_odd, high, low))
    return tables


def depth_kernel(values, from_right, from_left, gains, forward, backward, coefficients, rebuilt, halo):
    nz, ny, _ = values.shape
    cells = nz * ny
    for at in range(0, cells, X):
        both = jnp.concatenate([from_right[:, at : at + X], from_left[:, at : at + X]], 0)
        both = jnp.concatenate([both, jnp.zeros((X - HALO, X), jnp.float32)], 0)
        z, y = at // ny, at % ny
        turned = both.T
        if ny >= X:
            halo[z, y : y + X, :] = turned
        else:
            for k in range(X // ny):
                halo[z + k, :, :] = turned[k * ny : (k + 1) * ny]
    lane = lax.broadcasted_iota(jnp.int32, (ROWS, X), 1)
    inner = gain_tables(gains, lane % 2 == 1)
    beyond = gain_tables(gains, ((lane < 4) & (lane % 2 == 1)) | ((lane >= 4) & (lane % 2 == 0)))

    def body(k, carry):
        rows = pl.ds(pl.multiple_of(k * ROWS, ROWS), ROWS)
        inside = values[:, rows, :].reshape(nz * ROWS, X)
        outside = halo[:, rows, :].reshape(nz * ROWS, X)
        lines = jnp.dot(
            jnp.concatenate([inside, outside], 1), forward[...],
            precision=lax.Precision.HIGHEST, preferred_element_type=jnp.float32,
        )
        parts = []
        for part, tables in ((0, inner), (1, beyond)):
            cut = lines[:, part * X : (part + 1) * X]
            registers = [cut[z * ROWS : (z + 1) * ROWS] for z in range(nz)]
            found, again = lift_depth(registers, *tables)
            if part == 0:
                for z in range(nz):
                    coefficients[z, rows, :] = found[z]
            parts.append(jnp.concatenate(again, 0))
        lines = jnp.dot(
            jnp.concatenate(parts, 1), backward[...],
            precision=lax.Precision.HIGHEST, preferred_element_type=jnp.float32,
        )
        rebuilt[:, rows, :] = lines.reshape(nz, ROWS, X)
        return carry

    lax.fori_loop(0, ny // ROWS, body, 0)


def depths(values, from_right, from_left, gains, forward, backward):
    shape = jax.ShapeDtypeStruct(values.shape, jnp.float32)
    return call(
        depth_kernel, (shape, shape), 6, [pltpu.VMEM(values.shape, jnp.float32)], "depth", smem=(3,)
    )(values, from_right, from_left, gains, forward, backward)


def per_device(blocks, field, gains):
    f32 = jnp.float32
    index = lax.axis_index("ba")
    forward = jnp.where(
        index == 0,
        jnp.asarray(analysis_matrix(True, blocks == 1), f32),
        jnp.where(
            index == blocks - 1,
            jnp.asarray(analysis_matrix(False, True), f32),
            jnp.asarray(analysis_matrix(False, False), f32),
        ),
    )
    backward = jnp.asarray(synthesis_matrix(), f32)
    edge_weights = jnp.asarray(edge_matrix(), f32)

    nz = lax.axis_size("aa")
    ny = field.shape[1]
    by_lines = columns(field.reshape(ny, X), True)
    by_depth = lax.all_to_all(by_lines.reshape(nz, ny // nz, X), "aa", 0, 0, tiled=True)
    to_left, to_right = edges_of(by_depth.reshape(ny, X), edge_weights)
    from_right = lax.ppermute(to_left, "ba", [(k, k - 1) for k in range(1, blocks)])
    from_left = lax.ppermute(to_right, "ba", [(k, k + 1) for k in range(blocks - 1)])
    coefficients, rebuilt = depths(
        by_depth, from_right, from_left, gains.reshape(8), forward, backward
    )
    rebuilt = lax.all_to_all(rebuilt, "aa", 0, 0, tiled=True)
    rebuilt = columns(rebuilt.reshape(ny, X), False)
    return coefficients, rebuilt.reshape(1, ny, X)


def solution(mesh):
    return jax.shard_map(
        functools.partial(per_device, mesh.shape["ba"]),
        mesh=mesh,
        in_specs=(P("aa", None, "ba"), P()),
        out_specs=(P(None, "aa", "ba"), P("aa", None, "ba")),
        check_vma=False,
    )
```

```python
import functools

import jax
import jax.numpy as jnp
import numpy as np
from jax import lax
from jax.experimental import pallas as pl
from jax.experimental.pallas import tpu as pltpu
from jax.sharding import PartitionSpec as P

PREDICT_FIRST = -1.586134342059924
UPDATE_FIRST = -0.052980118572961
PREDICT_SECOND = 0.882911075530934
UPDATE_SECOND = 0.443506852043971
BALANCE = 1.230174104914001
A, B, C, E = PREDICT_FIRST, UPDATE_FIRST, PREDICT_SECOND, UPDATE_SECOND

X = 128
HALF = X // 2
ROWS = 8
MARGIN = 16
CHUNK = 256
VMEM_LIMIT = 24 * 1024 * 1024
EDGE = 8
HIGHEST = lax.Precision.HIGHEST


def edge_matrix():
    unit = np.eye(X)
    s, d = unit[0::2], unit[1::2]
    d1 = [d[n] + A * (s[n] + s[n + 1]) for n in range(HALF - 1)]
    s1 = [None] + [s[n] + B * (d1[n - 1] + d1[n]) for n in range(1, HALF - 1)]
    last = HALF - 1
    out = np.zeros((16, X))
    out[0] = s[0]
    out[1] = d1[0]
    out[2] = s1[1]
    out[3] = d1[1] + C * (s1[1] + s1[2])
    out[4] = d[last] + A * s[last]
    out[5] = s[last] + B * d1[last - 1]
    out[6] = d1[last - 1] + C * s1[last - 1]
    out[8] = d[0] + A * s[1]
    out[9] = s[1] + B * d1[1]
    out[10] = d1[1] + C * s1[2]
    out[12] = s[last]
    out[13] = d1[last - 1]
    out[14] = s1[last - 1]
    out[15] = d1[last - 2] + C * (s1[last - 2] + s1[last - 1])
    return np.concatenate([out[:, :EDGE], out[:, X - EDGE :]], 1)


def correction_matrix(left_end, right_end):
    unit = np.eye(24)
    own = unit[8:]
    h0, h1, h2, h3 = own[12:16] if right_end else unit[0:4]
    hp, hq, hr = own[8:11] if left_end else unit[4:7]
    s0, d10, p, q = own[0], own[1], own[4], own[5]
    add_d1 = A * h0
    d1 = p + add_d1
    s1_next = h0 + B * (d1 + h1)
    add_s1 = B * add_d1
    add_d2 = add_d1 + C * (add_s1 + s1_next)
    add_d2_before = C * add_s1
    add_s2 = add_s1 + E * (add_d2_before + add_d2)
    add_s2_before = E * add_d2_before
    s1 = q + B * d1
    d2 = d1 + C * (s1 + s1_next)
    d2_next = h1 + C * (s1_next + h2)
    s2_next = s1_next + E * (d2 + d2_next)
    s2_after = h2 + E * (d2_next + h3)
    right = [add_s2_before, add_d2_before, add_s2, add_d2]
    right_beyond = [s2_next, d2_next, s2_after, h3]
    d1_out = hp + A * s0
    s1_out = hq + B * d1_out
    add_s1 = B * d1_out
    s1 = s0 + B * (d1_out + d10)
    add_d2 = C * add_s1
    d2_out = d1_out + C * (s1_out + s1)
    d2_far = hr + C * s1_out
    s2_out = s1_out + E * (d2_far + d2_out)
    left = [add_s1 + E * (d2_out + add_d2), add_d2, E * add_d2, 0 * s0]
    left_beyond = [d2_out, s2_out, d2_far, 0 * s0]
    found = np.stack(left + right + right_beyond + left_beyond)
    return np.concatenate([found[:, :8], found[:, 8:] @ edge_matrix()], 1)


def own_analysis_matrix():
    unit = np.eye(X)
    zero = np.zeros((1, X))
    s, d = unit[0::2], unit[1::2]
    d = d + A * (s + np.concatenate([s[1:], zero]))
    s = s + B * (d + np.concatenate([zero, d[:-1]]))
    d = d + C * (s + np.concatenate([s[1:], zero]))
    s = s + E * (d + np.concatenate([zero, d[:-1]]))
    out = np.zeros((X, X))
    out[:, 0::2] = s.T
    out[:, 1::2] = d.T
    return out


def synthesis_matrix():
    unit = np.eye(X + 8)
    place = {k: k for k in range(X + 4)}
    place.update({-1: X + 4, -2: X + 5, -3: X + 6})
    n_all = HALF
    s2 = {n: unit[place[2 * n]] for n in range(-1, n_all + 2)}
    d2 = {n: unit[place[2 * n + 1]] for n in range(-2, n_all + 2)}
    s1 = {n: s2[n] - E * (d2[n - 1] + d2[n]) for n in range(-1, n_all + 2)}
    d1 = {n: d2[n] - C * (s1[n] + s1[n + 1]) for n in range(-1, n_all + 1)}
    s = {n: s1[n] - B * (d1[n - 1] + d1[n]) for n in range(n_all + 1)}
    d = {n: d1[n] - A * (s[n] + s[n + 1]) for n in range(n_all)}
    cells = np.zeros((X, X + 8))
    cells[0::2] = [s[n] for n in range(n_all)]
    cells[1::2] = [d[n] for n in range(n_all)]
    return cells


def edge_synthesis_matrix():
    inside = [0, 1, 2, 3, 124, 125, 126, 127] + [X + k for k in range(8)]
    return synthesis_matrix()[list(range(8)) + list(range(120, 128))][:, inside]


def call(kernel, out_shape, spaces, scratch=(), name=None, out_space=pltpu.VMEM, cost=None):
    if isinstance(out_space, tuple):
        out_specs = tuple(pl.BlockSpec(memory_space=space) for space in out_space)
    else:
        out_specs = jax.tree.map(lambda _: pl.BlockSpec(memory_space=out_space), out_shape)
    return pl.pallas_call(
        kernel,
        out_shape=out_shape,
        in_specs=[pl.BlockSpec(memory_space=space) for space in spaces],
        out_specs=out_specs,
        scratch_shapes=list(scratch),
        compiler_params=pltpu.CompilerParams(vmem_limit_bytes=VMEM_LIMIT),
        cost_estimate=cost,
        name=name,
    )


def array(*shape):
    return jax.ShapeDtypeStruct(shape, jnp.float32)


def after(rows):
    return pltpu.roll(rows, rows.shape[0] - 1, 0)


def before(rows):
    return pltpu.roll(rows, 1, 0)


def lift_rows(line, target, at, forward):
    cells = 128
    pairs = cells // 2
    wide = pairs + 8
    s = line[pl.ds(MARGIN + at - 8, wide, stride=2), :]
    d = line[pl.ds(MARGIN + at - 7, wide, stride=2), :]
    if forward:
        d = d + A * (s + after(s))
        s = s + B * (before(d) + d)
        d = d + C * (s + after(s))
        s = s + E * (before(d) + d)
        s = s * (1.0 / BALANCE)
        d = d * BALANCE
    else:
        s = s * BALANCE
        d = d * (1.0 / BALANCE)
        s = s - E * (before(d) + d)
        d = d - C * (s + after(s))
        s = s - B * (before(d) + d)
        d = d - A * (s + after(s))
    target[pl.ds(at, pairs, stride=2), :] = s[4 : 4 + pairs]
    target[pl.ds(at + 1, pairs, stride=2), :] = d[4 : 4 + pairs]


def mirror_start(line):
    for k in range(1, 9):
        line[pl.ds(MARGIN - k, 1), :] = line[pl.ds(MARGIN + k, 1), :]


def mirror_end(line, ny):
    for k in range(1, 9):
        line[pl.ds(MARGIN + ny - 1 + k, 1), :] = line[pl.ds(MARGIN + ny - 1 - k, 1), :]


def analyse_kernel(source, target, line, arrived):
    ny = source.shape[0]
    n = ny // CHUNK
    copies = []
    for k in range(n):
        inner = pl.ds(MARGIN + k * CHUNK, CHUNK)
        rows = pl.ds(k * CHUNK, CHUNK)
        copies.append(pltpu.make_async_copy(source.at[rows], line.at[inner], arrived.at[k]))
        copies[k].start()
    copies[0].wait()
    mirror_start(line)
    for k in range(n):
        if k + 1 < n:
            copies[k + 1].wait()
        else:
            mirror_end(line, ny)
        for at in range(k * CHUNK, (k + 1) * CHUNK, 128):
            lift_rows(line, target, at, True)


def analyse_columns(values):
    ny = values.shape[0]
    scratch = [
        pltpu.VMEM((ny + 2 * MARGIN, X), jnp.float32),
        pltpu.SemaphoreType.DMA((ny // CHUNK,)),
    ]
    return call(analyse_kernel, pltpu.VMEM((ny, X), jnp.float32), [pltpu.HBM], scratch, "analyse_y")(pltpu.with_memory_space_constraint(values, pltpu.HBM))


def synthesise_kernel(source, target, line, lifted, left):
    ny = source.shape[0]
    n = ny // CHUNK
    for k in range(n):
        line[pl.ds(MARGIN + k * CHUNK, CHUNK), :] = source[pl.ds(k * CHUNK, CHUNK), :]
    mirror_start(line)
    mirror_end(line, ny)
    copies = []
    for k in range(n):
        for at in range(k * CHUNK, (k + 1) * CHUNK, 128):
            lift_rows(line, lifted, at, False)
        rows = pl.ds(k * CHUNK, CHUNK)
        copies.append(pltpu.make_async_copy(lifted.at[rows], target.at[rows], left.at[k]))
        copies[k].start()
    for copy in copies:
        copy.wait()


def synthesise_columns(values):
    ny = values.shape[0]
    scratch = [
        pltpu.VMEM((ny + 2 * MARGIN, X), jnp.float32),
        pltpu.VMEM((ny, X), jnp.float32),
        pltpu.SemaphoreType.DMA((ny // CHUNK,)),
    ]
    return call(
        synthesise_kernel, array(ny, X), [pltpu.VMEM], scratch, "synthesise_y", pltpu.HBM
    )(values)


def edge_kernel(values, to_left, to_right, edges):
    cells = values.shape[0]
    for at in range(0, cells, X):
        turned = values[pl.ds(at, X), :].T
        edges[0:EDGE, pl.ds(at, X)] = turned[:EDGE]
        edges[EDGE : 2 * EDGE, pl.ds(at, X)] = turned[X - EDGE :]

    def cell(k):
        return edges[pl.ds(k, 1), :]

    s = [cell(2 * n) for n in range(EDGE)]
    d = [cell(2 * n + 1) for n in range(EDGE)]
    d1 = {n: d[n] + A * (s[n] + s[n + 1]) for n in (0, 1, 2, 5, 6)}
    s1 = {n: s[n] + B * (d1[n - 1] + d1[n]) for n in (1, 2, 6)}
    to_left[0:1] = s[0]
    to_left[1:2] = d1[0]
    to_left[2:3] = s1[1]
    to_left[3:4] = d1[1] + C * (s1[1] + s1[2])
    to_right[0:1] = d[7] + A * s[7]
    to_right[1:2] = s[7] + B * d1[6]
    to_right[2:3] = d1[6] + C * s1[6]
    to_right[3:4] = jnp.zeros_like(s[0])


def edges_of(values):
    cells = values.shape[0]
    shapes = (array(4, cells), array(4, cells), array(2 * EDGE, cells))
    return call(edge_kernel, shapes, [pltpu.VMEM], name="edges_x")(values)


def analyse_depth(cells):
    n = len(cells) // 2
    s, d = cells[0::2], cells[1::2]

    def right(k):
        return s[min(k + 1, n - 1)]

    def left(k):
        return d[max(k - 1, 0)]

    d = [d[k] + A * (s[k] + right(k)) for k in range(n)]
    s = [s[k] + B * (left(k) + d[k]) for k in range(n)]
    d = [d[k] + C * (s[k] + right(k)) for k in range(n)]
    s = [s[k] + E * (left(k) + d[k]) for k in range(n)]
    return s, d


def synthesise_depth(s, d):
    n = len(s)

    def right(k):
        return s[min(k + 1, n - 1)]

    def left(k):
        return d[max(k - 1, 0)]

    s = [s[k] - E * (left(k) + d[k]) for k in range(n)]
    d = [d[k] - C * (s[k] + right(k)) for k in range(n)]
    s = [s[k] - B * (left(k) + d[k]) for k in range(n)]
    d = [d[k] - A * (s[k] + right(k)) for k in range(n)]
    return [v for pair in zip(s, d) for v in pair]


def gain_tables(gains, y_odd, x_odd):
    tables = []
    for z in range(2):
        low = jnp.where(x_odd, gains[z, 0, 1], gains[z, 0, 0])
        high = jnp.where(x_odd, gains[z, 1, 1], gains[z, 1, 0])
        tables.append(jnp.where(y_odd, high, low))
    return tables


def scale_tables(x_odd):
    along = jnp.where(x_odd, BALANCE, 1.0 / BALANCE)
    return along * (1.0 / BALANCE), along * BALANCE


def dot(left, right):
    return jnp.dot(left, right, precision=lax.Precision.HIGHEST, preferred_element_type=jnp.float32)


def main_kernel(values, gains, edges, forward, backward, coefficients, rebuilt):
    del edges
    nz, ny, _ = values.shape
    lane = lax.broadcasted_iota(jnp.int32, (ROWS, X), 1)
    row = lax.broadcasted_iota(jnp.int32, (ROWS, X), 0)
    gain_low, gain_high = gain_tables(gains, row % 2 == 1, lane % 2 == 1)
    scale_low, scale_high = scale_tables(lane % 2 == 1)
    rebuilt[...] = dot(values[...].reshape(nz * ny, X), forward[...]).reshape(nz, ny, X)

    def body(k, carry):
        rows = pl.ds(pl.multiple_of(k * ROWS, ROWS), ROWS)
        s, d = analyse_depth([rebuilt[z, rows, :] for z in range(nz)])
        for n in range(nz // 2):
            coefficients[2 * n, rows, :] = s[n] * scale_low
            coefficients[2 * n + 1, rows, :] = d[n] * scale_high
        cells = synthesise_depth([v * gain_low for v in s], [v * gain_high for v in d])
        for z in range(nz):
            rebuilt[z, rows, :] = cells[z]
        return carry

    lax.fori_loop(0, ny // ROWS, body, 0)
    rebuilt[...] = dot(rebuilt[...].reshape(nz * ny, X), backward[...]).reshape(nz, ny, X)


def main_depths(values, gains, edges):
    shape = array(*values.shape)
    size = values.size
    cost = pl.CostEstimate(flops=100 * size, bytes_accessed=12 * size, transcendentals=0)
    spaces = [pltpu.VMEM, pltpu.SMEM, pl.ANY, pltpu.VMEM, pltpu.VMEM]
    forward = jnp.asarray(own_analysis_matrix(), jnp.float32)
    backward = jnp.asarray(synthesis_matrix()[:, :X].T, jnp.float32)
    return call(main_kernel, (shape, shape), spaces, name="depth_main", cost=cost)(
        values, gains, edges, forward, backward
    )


def halo_kernel(
    blocks, own_rebuilt, from_right, from_left, edges, gains, weights, spread, rebuilt, added, held, left
):
    nz = own_rebuilt.shape[0]
    index = lax.axis_index("ba")
    kind = 2 * (index == 0).astype(jnp.int32) + (index == blocks - 1).astype(jnp.int32)
    halo = jnp.concatenate([from_right[...], from_left[...], edges[...]], 0)
    found = dot(weights[kind], halo)
    lane = lax.broadcasted_iota(jnp.int32, (ROWS, X), 1)
    row = lax.broadcasted_iota(jnp.int32, (ROWS, X), 0)
    low = lane < HALF
    low_16 = lax.broadcasted_iota(jnp.int32, (16, X), 1) < HALF
    cells = []
    for k in range(nz // 2):
        inside = found[0:8, k * X : (k + 1) * X]
        beyond = found[8:16, k * X : (k + 1) * X]
        cells.append(jnp.where(low, inside, pltpu.roll(beyond, HALF, 1)))
        cells.append(jnp.where(low, pltpu.roll(inside, HALF, 1), beyond))
    x_odd = (row + jnp.where(low | (row < 4), 0, 1)) % 2 == 1
    gain_low, gain_high = gain_tables(gains, lane % 2 == 1, x_odd)
    scale_low, scale_high = scale_tables(x_odd)
    s, d = analyse_depth(cells)
    for n in range(nz // 2):
        added[2 * n] = s[n] * scale_low
        added[2 * n + 1] = d[n] * scale_high
    copies = []
    cells = synthesise_depth([v * gain_low for v in s], [v * gain_high for v in d])
    table = [spread[:, k * X : (k + 1) * X] for k in range(8)]
    middle = jnp.zeros((X - 16, X), jnp.float32)
    for k in range(nz // 2):
        mixed = []
        for v in cells[2 * k : 2 * k + 2]:
            total = None
            for m in range(8):
                term = table[m] * jnp.broadcast_to(v[m : m + 1], (16, X))
                total = term if total is None else total + term
            mixed.append(total + pltpu.roll(total, HALF, 1))
        both = jnp.where(low_16, *mixed)
        turned = jnp.concatenate([both[:8], middle, both[8:]], 0).T
        held[2 * k] = own_rebuilt[2 * k] + turned[:HALF]
        held[2 * k + 1] = own_rebuilt[2 * k + 1] + turned[HALF:]
        if k % 2 == 1:
            part = pl.ds(2 * k - 2, 4)
            copies.append(pltpu.make_async_copy(held.at[part], rebuilt.at[part], left.at[k // 2]))
            copies[-1].start()
    for copy in copies:
        copy.wait()


def add_halo(blocks, own_rebuilt, from_right, from_left, edges, gains):
    nz = own_rebuilt.shape[0]
    kinds = [correction_matrix(left, right) for left in (False, True) for right in (False, True)]
    mixing = edge_synthesis_matrix()
    spread = np.zeros((16, 8, X))
    spread[:, :, :HALF] = mixing[:, :8, None]
    spread[:, :, HALF:] = mixing[:, 8:, None]
    shapes = (array(*own_rebuilt.shape), array(nz, ROWS, X))
    spaces = [pltpu.VMEM] * 4 + [pltpu.SMEM] + [pltpu.VMEM] * 2
    scratch = [
        pltpu.VMEM(own_rebuilt.shape, jnp.float32),
        pltpu.SemaphoreType.DMA((nz // 4,)),
    ]
    kernel = functools.partial(halo_kernel, blocks)
    out_space = (pl.ANY, pltpu.VMEM)
    return call(kernel, shapes, spaces, scratch, "depth_halo", out_space)(
        own_rebuilt, from_right, from_left, edges, gains,
        jnp.asarray(np.stack(kinds), jnp.float32), jnp.asarray(spread.reshape(16, 8 * X), jnp.float32),
    )


def finish_kernel(own, added, coefficients):
    nz = own.shape[0]
    low = lax.broadcasted_iota(jnp.int32, (ROWS, X), 1) < HALF
    row = lax.broadcasted_iota(jnp.int32, (ROWS, X), 0)
    middle = jnp.zeros((X - 16, X), jnp.float32)
    for k in range(nz // 2):
        both = jnp.where(low, added[2 * k], pltpu.roll(added[2 * k + 1], HALF, 1))
        ends = [jnp.where(row < 4, both, 0.0), middle, jnp.where(row < 4, 0.0, both)]
        turned = jnp.concatenate(ends, 0).T
        coefficients[2 * k] = own[2 * k] + turned[:HALF]
        coefficients[2 * k + 1] = own[2 * k + 1] + turned[HALF:]


def finish(own, added):
    size = own.size
    cost = pl.CostEstimate(flops=10 * size, bytes_accessed=8 * size, transcendentals=0)
    return call(
        finish_kernel, array(*own.shape), [pltpu.VMEM] * 2, name="coefficients_halo", cost=cost
    )(own, added)


def per_device(blocks, field, gains):
    nz = lax.axis_size("aa")
    ny = field.shape[1]
    by_lines = analyse_columns(field.reshape(ny, X))
    by_depth = lax.all_to_all(by_lines.reshape(nz, ny // nz, X), "aa", 0, 0, tiled=True)
    to_left, to_right, edges = edges_of(by_depth.reshape(ny, X))
    from_right = lax.ppermute(to_left, "ba", [(k, k - 1) for k in range(1, blocks)])
    from_left = lax.ppermute(to_right, "ba", [(k, k + 1) for k in range(blocks - 1)])
    own_coefficients, own_rebuilt = main_depths(by_depth, gains, edges)
    rebuilt, added = add_halo(blocks, own_rebuilt, from_right, from_left, edges, gains)
    coefficients = finish(own_coefficients, added)
    rebuilt = lax.all_to_all(rebuilt, "aa", 0, 0, tiled=True)
    rebuilt = synthesise_columns(rebuilt.reshape(ny, X))
    return coefficients, rebuilt.reshape(1, ny, X)


def solution(mesh):
    return jax.shard_map(
        functools.partial(per_device, mesh.shape["ba"]),
        mesh=mesh,
        in_specs=(P("aa", None, "ba"), P()),
        out_specs=(P(None, "aa", "ba"), P("aa", None, "ba")),
        check_vma=False,
    )
```

```python
import functools

import jax
import jax.numpy as jnp
import numpy as np
from jax import lax
from jax.experimental import pallas as pl
from jax.experimental.pallas import tpu as pltpu
from jax.sharding import PartitionSpec as P

PREDICT_FIRST = -1.586134342059924
UPDATE_FIRST = -0.052980118572961
PREDICT_SECOND = 0.882911075530934
UPDATE_SECOND = 0.443506852043971
BALANCE = 1.230174104914001
A, B, C, E = PREDICT_FIRST, UPDATE_FIRST, PREDICT_SECOND, UPDATE_SECOND

X = 128
HALF = X // 2
ROWS = 8
MARGIN = 16
CHUNK = 256
VMEM_LIMIT = 24 * 1024 * 1024
EDGE = 8
HIGHEST = lax.Precision.HIGHEST

def exchange_order(n):
    if n != 32:
        return [(k + 2) % n for k in range(n)]

    def where(k):
        return k // 8, k // 2 % 4, k % 2

    first = 2

    def distance(k):
        (x, y, core), (x_first, y_first, core_first) = where(k), where(first)
        along = abs(x - x_first)
        return 10 * (min(along, 4 - along) + abs(y - y_first)) + (core != core_first)

    rest = [k for k in range(n) if k != first]
    return [first, *sorted(rest, key=lambda k: -distance(k))]


def places(order):
    out = [0] * len(order)
    for k, device in enumerate(order):
        out[device] = k
    return out


def edge_matrix():
    unit = np.eye(X)
    s, d = unit[0::2], unit[1::2]
    d1 = [d[n] + A * (s[n] + s[n + 1]) for n in range(HALF - 1)]
    s1 = [None] + [s[n] + B * (d1[n - 1] + d1[n]) for n in range(1, HALF - 1)]
    last = HALF - 1
    out = np.zeros((16, X))
    out[0] = s[0]
    out[1] = d1[0]
    out[2] = s1[1]
    out[3] = d1[1] + C * (s1[1] + s1[2])
    out[4] = d[last] + A * s[last]
    out[5] = s[last] + B * d1[last - 1]
    out[6] = d1[last - 1] + C * s1[last - 1]
    out[8] = d[0] + A * s[1]
    out[9] = s[1] + B * d1[1]
    out[10] = d1[1] + C * s1[2]
    out[12] = s[last]
    out[13] = d1[last - 1]
    out[14] = s1[last - 1]
    out[15] = d1[last - 2] + C * (s1[last - 2] + s1[last - 1])
    return np.concatenate([out[:, :EDGE], out[:, X - EDGE :]], 1)


def correction_matrix(left_end, right_end):
    unit = np.eye(24)
    own = unit[8:]
    h0, h1, h2, h3 = own[12:16] if right_end else unit[0:4]
    hp, hq, hr = own[8:11] if left_end else unit[4:7]
    s0, d10, p, q = own[0], own[1], own[4], own[5]
    add_d1 = A * h0
    d1 = p + add_d1
    s1_next = h0 + B * (d1 + h1)
    add_s1 = B * add_d1
    add_d2 = add_d1 + C * (add_s1 + s1_next)
    add_d2_before = C * add_s1
    add_s2 = add_s1 + E * (add_d2_before + add_d2)
    add_s2_before = E * add_d2_before
    s1 = q + B * d1
    d2 = d1 + C * (s1 + s1_next)
    d2_next = h1 + C * (s1_next + h2)
    s2_next = s1_next + E * (d2 + d2_next)
    s2_after = h2 + E * (d2_next + h3)
    right = [add_s2_before, add_d2_before, add_s2, add_d2]
    right_beyond = [s2_next, d2_next, s2_after, h3]
    d1_out = hp + A * s0
    s1_out = hq + B * d1_out
    add_s1 = B * d1_out
    s1 = s0 + B * (d1_out + d10)
    add_d2 = C * add_s1
    d2_out = d1_out + C * (s1_out + s1)
    d2_far = hr + C * s1_out
    s2_out = s1_out + E * (d2_far + d2_out)
    left = [add_s1 + E * (d2_out + add_d2), add_d2, E * add_d2, 0 * s0]
    left_beyond = [d2_out, s2_out, d2_far, 0 * s0]
    found = np.stack(left + right + right_beyond + left_beyond)
    return np.concatenate([found[:, :8], found[:, 8:] @ edge_matrix()], 1)


def own_analysis_matrix():
    unit = np.eye(X)
    zero = np.zeros((1, X))
    s, d = unit[0::2], unit[1::2]
    d = d + A * (s + np.concatenate([s[1:], zero]))
    s = s + B * (d + np.concatenate([zero, d[:-1]]))
    d = d + C * (s + np.concatenate([s[1:], zero]))
    s = s + E * (d + np.concatenate([zero, d[:-1]]))
    out = np.zeros((X, X))
    out[:, 0::2] = s.T
    out[:, 1::2] = d.T
    return out


def synthesis_matrix():
    unit = np.eye(X + 8)
    place = {k: k for k in range(X + 4)}
    place.update({-1: X + 4, -2: X + 5, -3: X + 6})
    n_all = HALF
    s2 = {n: unit[place[2 * n]] for n in range(-1, n_all + 2)}
    d2 = {n: unit[place[2 * n + 1]] for n in range(-2, n_all + 2)}
    s1 = {n: s2[n] - E * (d2[n - 1] + d2[n]) for n in range(-1, n_all + 2)}
    d1 = {n: d2[n] - C * (s1[n] + s1[n + 1]) for n in range(-1, n_all + 1)}
    s = {n: s1[n] - B * (d1[n - 1] + d1[n]) for n in range(n_all + 1)}
    d = {n: d1[n] - A * (s[n] + s[n + 1]) for n in range(n_all)}
    cells = np.zeros((X, X + 8))
    cells[0::2] = [s[n] for n in range(n_all)]
    cells[1::2] = [d[n] for n in range(n_all)]
    return cells


def edge_synthesis_matrix():
    inside = [0, 1, 2, 3, 124, 125, 126, 127] + [X + k for k in range(8)]
    return synthesis_matrix()[list(range(8)) + list(range(120, 128))][:, inside]


def call(kernel, out_shape, spaces, scratch=(), name=None, out_space=pltpu.VMEM, cost=None):
    if isinstance(out_space, tuple):
        out_specs = tuple(pl.BlockSpec(memory_space=space) for space in out_space)
    else:
        out_specs = jax.tree.map(lambda _: pl.BlockSpec(memory_space=out_space), out_shape)
    return pl.pallas_call(
        kernel,
        out_shape=out_shape,
        in_specs=[pl.BlockSpec(memory_space=space) for space in spaces],
        out_specs=out_specs,
        scratch_shapes=list(scratch),
        compiler_params=pltpu.CompilerParams(vmem_limit_bytes=VMEM_LIMIT),
        cost_estimate=cost,
        name=name,
    )


def array(*shape):
    return jax.ShapeDtypeStruct(shape, jnp.float32)


def after(rows):
    return pltpu.roll(rows, rows.shape[0] - 1, 0)


def before(rows):
    return pltpu.roll(rows, 1, 0)


def lift_rows(line, target, at, forward, place):
    cells = 128
    pairs = cells // 2
    wide = pairs + 8
    s = line[pl.ds(MARGIN + at - 8, wide, stride=2), :]
    d = line[pl.ds(MARGIN + at - 7, wide, stride=2), :]
    if forward:
        d = d + A * (s + after(s))
        s = s + B * (before(d) + d)
        d = d + C * (s + after(s))
        s = s + E * (before(d) + d)
        s = s * (1.0 / BALANCE)
        d = d * BALANCE
    else:
        s = s * BALANCE
        d = d * (1.0 / BALANCE)
        s = s - E * (before(d) + d)
        d = d - C * (s + after(s))
        s = s - B * (before(d) + d)
        d = d - A * (s + after(s))
    block = target.shape[0] // len(place)
    half = block // 2
    for k in range(cells // block):
        to = place[at // block + k] * block
        target[pl.ds(to, half, stride=2), :] = s[4 + k * half : 4 + (k + 1) * half]
        target[pl.ds(to + 1, half, stride=2), :] = d[4 + k * half : 4 + (k + 1) * half]


def mirror_start(line):
    for k in range(1, 9):
        line[pl.ds(MARGIN - k, 1), :] = line[pl.ds(MARGIN + k, 1), :]


def mirror_end(line, ny):
    for k in range(1, 9):
        line[pl.ds(MARGIN + ny - 1 + k, 1), :] = line[pl.ds(MARGIN + ny - 1 - k, 1), :]


def analyse_kernel(order, source, target, line, arrived):
    ny = source.shape[0]
    n = ny // CHUNK
    copies = []
    for k in range(n):
        inner = pl.ds(MARGIN + k * CHUNK, CHUNK)
        rows = pl.ds(k * CHUNK, CHUNK)
        copies.append(pltpu.make_async_copy(source.at[rows], line.at[inner], arrived.at[k]))
        copies[k].start()
    copies[0].wait()
    mirror_start(line)
    for k in range(n):
        if k + 1 < n:
            copies[k + 1].wait()
        else:
            mirror_end(line, ny)
        for at in range(k * CHUNK, (k + 1) * CHUNK, 128):
            lift_rows(line, target, at, True, places(order))


def analyse_columns(order, values):
    ny = values.shape[0]
    values = pltpu.with_memory_space_constraint(values, pltpu.HBM)
    scratch = [
        pltpu.VMEM((ny + 2 * MARGIN, X), jnp.float32),
        pltpu.SemaphoreType.DMA((ny // CHUNK,)),
    ]
    out_shape = pltpu.VMEM((ny, X), jnp.float32)
    kernel = functools.partial(analyse_kernel, order)
    return call(kernel, out_shape, [pltpu.HBM], scratch, "analyse_y")(values)


def synthesise_kernel(order, source, target, line, lifted, left):
    ny = source.shape[0]
    n = ny // CHUNK
    block = ny // len(order)
    for k, device in enumerate(order):
        line[pl.ds(MARGIN + device * block, block), :] = source[pl.ds(k * block, block), :]
    mirror_start(line)
    mirror_end(line, ny)
    copies = []
    for k in range(n):
        for at in range(k * CHUNK, (k + 1) * CHUNK, 128):
            lift_rows(line, lifted, at, False, range(len(order)))
        rows = pl.ds(k * CHUNK, CHUNK)
        copies.append(pltpu.make_async_copy(lifted.at[rows], target.at[rows], left.at[k]))
        copies[k].start()
    for copy in copies:
        copy.wait()


def synthesise_columns(order, values):
    ny = values.shape[0]
    scratch = [
        pltpu.VMEM((ny + 2 * MARGIN, X), jnp.float32),
        pltpu.VMEM((ny, X), jnp.float32),
        pltpu.SemaphoreType.DMA((ny // CHUNK,)),
    ]
    kernel = functools.partial(synthesise_kernel, order)
    return call(kernel, array(ny, X), [pltpu.VMEM], scratch, "synthesise_y", pltpu.HBM)(values)


def edge_kernel(values, to_left, to_right, edges):
    cells = values.shape[0]
    for at in range(0, cells, X):
        turned = values[pl.ds(at, X), :].T
        edges[0:EDGE, pl.ds(at, X)] = turned[:EDGE]
        edges[EDGE : 2 * EDGE, pl.ds(at, X)] = turned[X - EDGE :]

    def cell(k):
        return edges[pl.ds(k, 1), :]

    s = [cell(2 * n) for n in range(EDGE)]
    d = [cell(2 * n + 1) for n in range(EDGE)]
    d1 = {n: d[n] + A * (s[n] + s[n + 1]) for n in (0, 1, 2, 5, 6)}
    s1 = {n: s[n] + B * (d1[n - 1] + d1[n]) for n in (1, 2, 6)}
    to_left[0:1] = s[0]
    to_left[1:2] = d1[0]
    to_left[2:3] = s1[1]
    to_left[3:4] = d1[1] + C * (s1[1] + s1[2])
    to_right[0:1] = d[7] + A * s[7]
    to_right[1:2] = s[7] + B * d1[6]
    to_right[2:3] = d1[6] + C * s1[6]
    to_right[3:4] = jnp.zeros_like(s[0])


def edges_of(values):
    cells = values.shape[0]
    shapes = (array(4, cells), array(4, cells), array(2 * EDGE, cells))
    return call(edge_kernel, shapes, [pltpu.VMEM], name="edges_x")(values)


def analyse_depth(cells):
    n = len(cells) // 2
    s, d = cells[0::2], cells[1::2]

    def right(k):
        return s[min(k + 1, n - 1)]

    def left(k):
        return d[max(k - 1, 0)]

    d = [d[k] + A * (s[k] + right(k)) for k in range(n)]
    s = [s[k] + B * (left(k) + d[k]) for k in range(n)]
    d = [d[k] + C * (s[k] + right(k)) for k in range(n)]
    s = [s[k] + E * (left(k) + d[k]) for k in range(n)]
    return s, d


def synthesise_depth(s, d):
    n = len(s)

    def right(k):
        return s[min(k + 1, n - 1)]

    def left(k):
        return d[max(k - 1, 0)]

    s = [s[k] - E * (left(k) + d[k]) for k in range(n)]
    d = [d[k] - C * (s[k] + right(k)) for k in range(n)]
    s = [s[k] - B * (left(k) + d[k]) for k in range(n)]
    d = [d[k] - A * (s[k] + right(k)) for k in range(n)]
    return [v for pair in zip(s, d) for v in pair]


def gain_tables(gains, y_odd, x_odd):
    tables = []
    for z in range(2):
        low = jnp.where(x_odd, gains[z, 0, 1], gains[z, 0, 0])
        high = jnp.where(x_odd, gains[z, 1, 1], gains[z, 1, 0])
        tables.append(jnp.where(y_odd, high, low))
    return tables


def scale_tables(x_odd):
    along = jnp.where(x_odd, BALANCE, 1.0 / BALANCE)
    return along * (1.0 / BALANCE), along * BALANCE


def dot(left, right):
    return jnp.dot(left, right, precision=lax.Precision.HIGHEST, preferred_element_type=jnp.float32)


def main_kernel(order, values, gains, edges, forward, backward, coefficients, rebuilt):
    del edges
    nz, ny, _ = values.shape
    place = places(order)
    lane = lax.broadcasted_iota(jnp.int32, (ROWS, X), 1)
    row = lax.broadcasted_iota(jnp.int32, (ROWS, X), 0)
    gain_low, gain_high = gain_tables(gains, row % 2 == 1, lane % 2 == 1)
    scale_low, scale_high = scale_tables(lane % 2 == 1)
    rebuilt[...] = dot(values[...].reshape(nz * ny, X), forward[...]).reshape(nz, ny, X)

    def body(k, carry):
        rows = pl.ds(pl.multiple_of(k * ROWS, ROWS), ROWS)
        s, d = analyse_depth([rebuilt[place[z], rows, :] for z in range(nz)])
        for n in range(nz // 2):
            coefficients[2 * n, rows, :] = s[n] * scale_low
            coefficients[2 * n + 1, rows, :] = d[n] * scale_high
        cells = synthesise_depth([v * gain_low for v in s], [v * gain_high for v in d])
        for z in range(nz):
            rebuilt[place[z], rows, :] = cells[z]
        return carry

    lax.fori_loop(0, ny // ROWS, body, 0)
    rebuilt[...] = dot(rebuilt[...].reshape(nz * ny, X), backward[...]).reshape(nz, ny, X)


def main_depths(order, values, gains, edges):
    shape = array(*values.shape)
    size = values.size
    cost = pl.CostEstimate(flops=100 * size, bytes_accessed=12 * size, transcendentals=0)
    spaces = [pltpu.VMEM, pltpu.SMEM, pl.ANY, pltpu.VMEM, pltpu.VMEM]
    forward = jnp.asarray(own_analysis_matrix(), jnp.float32)
    backward = jnp.asarray(synthesis_matrix()[:, :X].T, jnp.float32)
    kernel = functools.partial(main_kernel, order)
    return call(kernel, (shape, shape), spaces, name="depth_main", cost=cost)(
        values, gains, edges, forward, backward
    )


def halo_kernel(
    blocks, order, own_rebuilt, from_right, from_left, edges, gains, weights, spread,
    rebuilt, added, held, left,
):
    nz = own_rebuilt.shape[0]
    index = lax.axis_index("ba")
    kind = 2 * (index == 0).astype(jnp.int32) + (index == blocks - 1).astype(jnp.int32)
    halo = jnp.concatenate([from_right[...], from_left[...], edges[...]], 0)
    found = dot(weights[kind], halo)
    lane = lax.broadcasted_iota(jnp.int32, (ROWS, X), 1)
    row = lax.broadcasted_iota(jnp.int32, (ROWS, X), 0)
    low = lane < HALF
    low_16 = lax.broadcasted_iota(jnp.int32, (16, X), 1) < HALF
    cells = []
    for k in range(nz // 2):
        inside = found[0:8, k * X : (k + 1) * X]
        beyond = found[8:16, k * X : (k + 1) * X]
        cells.append(jnp.where(low, inside, pltpu.roll(beyond, HALF, 1)))
        cells.append(jnp.where(low, pltpu.roll(inside, HALF, 1), beyond))
    x_odd = (row + jnp.where(low | (row < 4), 0, 1)) % 2 == 1
    gain_low, gain_high = gain_tables(gains, lane % 2 == 1, x_odd)
    scale_low, scale_high = scale_tables(x_odd)
    s, d = analyse_depth([cells[k] for k in places(order)])
    for n in range(nz // 2):
        added[2 * n] = s[n] * scale_low
        added[2 * n + 1] = d[n] * scale_high
    copies = []
    cells = synthesise_depth([v * gain_low for v in s], [v * gain_high for v in d])
    table = [spread[:, k * X : (k + 1) * X] for k in range(8)]
    middle = jnp.zeros((X - 16, X), jnp.float32)
    for k in range(nz // 2):
        mixed = []
        for v in (cells[order[2 * k]], cells[order[2 * k + 1]]):
            total = None
            for m in range(8):
                term = table[m] * jnp.broadcast_to(v[m : m + 1], (16, X))
                total = term if total is None else total + term
            mixed.append(total + pltpu.roll(total, HALF, 1))
        both = jnp.where(low_16, *mixed)
        turned = jnp.concatenate([both[:8], middle, both[8:]], 0).T
        held[2 * k] = own_rebuilt[2 * k] + turned[:HALF]
        held[2 * k + 1] = own_rebuilt[2 * k + 1] + turned[HALF:]
        if k % 2 == 1:
            part = pl.ds(2 * k - 2, 4)
            copies.append(pltpu.make_async_copy(held.at[part], rebuilt.at[part], left.at[k // 2]))
            copies[-1].start()
    for copy in copies:
        copy.wait()


def add_halo(blocks, order, own_rebuilt, from_right, from_left, edges, gains):
    nz = own_rebuilt.shape[0]
    kinds = [correction_matrix(left, right) for left in (False, True) for right in (False, True)]
    mixing = edge_synthesis_matrix()
    spread = np.zeros((16, 8, X))
    spread[:, :, :HALF] = mixing[:, :8, None]
    spread[:, :, HALF:] = mixing[:, 8:, None]
    shapes = (array(*own_rebuilt.shape), array(nz, ROWS, X))
    spaces = [pltpu.VMEM] * 4 + [pltpu.SMEM] + [pltpu.VMEM] * 2
    scratch = [
        pltpu.VMEM(own_rebuilt.shape, jnp.float32),
        pltpu.SemaphoreType.DMA((nz // 4,)),
    ]
    kernel = functools.partial(halo_kernel, blocks, order)
    out_space = (pl.ANY, pltpu.VMEM)
    return call(kernel, shapes, spaces, scratch, "depth_halo", out_space)(
        own_rebuilt, from_right, from_left, edges, gains,
        jnp.asarray(np.stack(kinds), jnp.float32), jnp.asarray(spread.reshape(16, 8 * X), jnp.float32),
    )


def finish_kernel(own, added, coefficients):
    nz = own.shape[0]
    low = lax.broadcasted_iota(jnp.int32, (ROWS, X), 1) < HALF
    row = lax.broadcasted_iota(jnp.int32, (ROWS, X), 0)
    middle = jnp.zeros((X - 16, X), jnp.float32)
    for k in range(nz // 2):
        both = jnp.where(low, added[2 * k], pltpu.roll(added[2 * k + 1], HALF, 1))
        ends = [jnp.where(row < 4, both, 0.0), middle, jnp.where(row < 4, 0.0, both)]
        turned = jnp.concatenate(ends, 0).T
        coefficients[2 * k] = own[2 * k] + turned[:HALF]
        coefficients[2 * k + 1] = own[2 * k + 1] + turned[HALF:]


def finish(own, added):
    size = own.size
    cost = pl.CostEstimate(flops=10 * size, bytes_accessed=8 * size, transcendentals=0)
    return call(
        finish_kernel, array(*own.shape), [pltpu.VMEM] * 2, name="coefficients_halo", cost=cost
    )(own, added)


def per_device(blocks, field, gains):
    nz = lax.axis_size("aa")
    ny = field.shape[1]
    order = exchange_order(nz)

    def exchange(blocks_):
        blocks_ = blocks_.reshape(nz, ny // nz, X)
        return lax.all_to_all(blocks_, "aa", 0, 0, axis_index_groups=[order], tiled=True)

    by_depth = exchange(analyse_columns(order, field.reshape(ny, X)))
    to_left, to_right, edges = edges_of(by_depth.reshape(ny, X))
    from_right = lax.ppermute(to_left, "ba", [(k, k - 1) for k in range(1, blocks)])
    from_left = lax.ppermute(to_right, "ba", [(k, k + 1) for k in range(blocks - 1)])
    own_coefficients, own_rebuilt = main_depths(order, by_depth, gains, edges)
    rebuilt, added = add_halo(blocks, order, own_rebuilt, from_right, from_left, edges, gains)
    coefficients = finish(own_coefficients, added)
    rebuilt = synthesise_columns(order, exchange(rebuilt).reshape(ny, X))
    return coefficients, rebuilt.reshape(1, ny, X)


def solution(mesh):
    return jax.shard_map(
        functools.partial(per_device, mesh.shape["ba"]),
        mesh=mesh,
        in_specs=(P("aa", None, "ba"), P()),
        out_specs=(P(None, "aa", "ba"), P("aa", None, "ba")),
        check_vma=False,
    )
```

```python
import functools

import jax
import jax.numpy as jnp
import numpy as np
from jax import lax
from jax.experimental import pallas as pl
from jax.experimental.pallas import tpu as pltpu
from jax.sharding import PartitionSpec as P

PREDICT_FIRST = -1.586134342059924
UPDATE_FIRST = -0.052980118572961
PREDICT_SECOND = 0.882911075530934
UPDATE_SECOND = 0.443506852043971
BALANCE = 1.230174104914001
A, B, C, E = PREDICT_FIRST, UPDATE_FIRST, PREDICT_SECOND, UPDATE_SECOND

X = 128
HALF = X // 2
ROWS = 8
MARGIN = 16
CHUNK = 256
VMEM_LIMIT = 24 * 1024 * 1024
EDGE = 8
HIGHEST = lax.Precision.HIGHEST

def exchange_order(n):
    if n != 32:
        return [(k + 2) % n for k in range(n)]

    def where(k):
        return k // 8, k // 2 % 4, k % 2

    first = 2

    def distance(k):
        (x, y, core), (x_first, y_first, core_first) = where(k), where(first)
        along = abs(x - x_first)
        return 10 * (min(along, 4 - along) + abs(y - y_first)) + (core != core_first)

    rest = [k for k in range(n) if k != first]
    return [first, *sorted(rest, key=lambda k: -distance(k))]


def places(order):
    out = [0] * len(order)
    for k, device in enumerate(order):
        out[device] = k
    return out


def edge_matrix():
    unit = np.eye(X)
    s, d = unit[0::2], unit[1::2]
    d1 = [d[n] + A * (s[n] + s[n + 1]) for n in range(HALF - 1)]
    s1 = [None] + [s[n] + B * (d1[n - 1] + d1[n]) for n in range(1, HALF - 1)]
    last = HALF - 1
    out = np.zeros((16, X))
    out[0] = s[0]
    out[1] = d1[0]
    out[2] = s1[1]
    out[3] = d1[1] + C * (s1[1] + s1[2])
    out[4] = d[last] + A * s[last]
    out[5] = s[last] + B * d1[last - 1]
    out[6] = d1[last - 1] + C * s1[last - 1]
    out[8] = d[0] + A * s[1]
    out[9] = s[1] + B * d1[1]
    out[10] = d1[1] + C * s1[2]
    out[12] = s[last]
    out[13] = d1[last - 1]
    out[14] = s1[last - 1]
    out[15] = d1[last - 2] + C * (s1[last - 2] + s1[last - 1])
    return np.concatenate([out[:, :EDGE], out[:, X - EDGE :]], 1)


def correction_matrix(left_end, right_end):
    unit = np.eye(24)
    own = unit[8:]
    h0, h1, h2, h3 = own[12:16] if right_end else unit[0:4]
    hp, hq, hr = own[8:11] if left_end else unit[4:7]
    s0, d10, p, q = own[0], own[1], own[4], own[5]
    add_d1 = A * h0
    d1 = p + add_d1
    s1_next = h0 + B * (d1 + h1)
    add_s1 = B * add_d1
    add_d2 = add_d1 + C * (add_s1 + s1_next)
    add_d2_before = C * add_s1
    add_s2 = add_s1 + E * (add_d2_before + add_d2)
    add_s2_before = E * add_d2_before
    s1 = q + B * d1
    d2 = d1 + C * (s1 + s1_next)
    d2_next = h1 + C * (s1_next + h2)
    s2_next = s1_next + E * (d2 + d2_next)
    s2_after = h2 + E * (d2_next + h3)
    right = [add_s2_before, add_d2_before, add_s2, add_d2]
    right_beyond = [s2_next, d2_next, s2_after, h3]
    d1_out = hp + A * s0
    s1_out = hq + B * d1_out
    add_s1 = B * d1_out
    s1 = s0 + B * (d1_out + d10)
    add_d2 = C * add_s1
    d2_out = d1_out + C * (s1_out + s1)
    d2_far = hr + C * s1_out
    s2_out = s1_out + E * (d2_far + d2_out)
    left = [add_s1 + E * (d2_out + add_d2), add_d2, E * add_d2, 0 * s0]
    left_beyond = [d2_out, s2_out, d2_far, 0 * s0]
    found = np.stack(left + right + right_beyond + left_beyond)
    return np.concatenate([found[:, :8], found[:, 8:] @ edge_matrix()], 1)


def own_analysis_matrix():
    unit = np.eye(X)
    zero = np.zeros((1, X))
    s, d = unit[0::2], unit[1::2]
    d = d + A * (s + np.concatenate([s[1:], zero]))
    s = s + B * (d + np.concatenate([zero, d[:-1]]))
    d = d + C * (s + np.concatenate([s[1:], zero]))
    s = s + E * (d + np.concatenate([zero, d[:-1]]))
    out = np.zeros((X, X))
    out[:, 0::2] = s.T
    out[:, 1::2] = d.T
    return out


def synthesis_matrix():
    unit = np.eye(X + 8)
    place = {k: k for k in range(X + 4)}
    place.update({-1: X + 4, -2: X + 5, -3: X + 6})
    n_all = HALF
    s2 = {n: unit[place[2 * n]] for n in range(-1, n_all + 2)}
    d2 = {n: unit[place[2 * n + 1]] for n in range(-2, n_all + 2)}
    s1 = {n: s2[n] - E * (d2[n - 1] + d2[n]) for n in range(-1, n_all + 2)}
    d1 = {n: d2[n] - C * (s1[n] + s1[n + 1]) for n in range(-1, n_all + 1)}
    s = {n: s1[n] - B * (d1[n - 1] + d1[n]) for n in range(n_all + 1)}
    d = {n: d1[n] - A * (s[n] + s[n + 1]) for n in range(n_all)}
    cells = np.zeros((X, X + 8))
    cells[0::2] = [s[n] for n in range(n_all)]
    cells[1::2] = [d[n] for n in range(n_all)]
    return cells


def edge_synthesis_matrix():
    inside = [0, 1, 2, 3, 124, 125, 126, 127] + [X + k for k in range(8)]
    return synthesis_matrix()[list(range(8)) + list(range(120, 128))][:, inside]


def call(kernel, out_shape, spaces, scratch=(), name=None, out_space=pltpu.VMEM, cost=None):
    if isinstance(out_space, tuple):
        out_specs = tuple(pl.BlockSpec(memory_space=space) for space in out_space)
    else:
        out_specs = jax.tree.map(lambda _: pl.BlockSpec(memory_space=out_space), out_shape)
    return pl.pallas_call(
        kernel,
        out_shape=out_shape,
        in_specs=[pl.BlockSpec(memory_space=space) for space in spaces],
        out_specs=out_specs,
        scratch_shapes=list(scratch),
        compiler_params=pltpu.CompilerParams(vmem_limit_bytes=VMEM_LIMIT),
        cost_estimate=cost,
        name=name,
    )


def array(*shape):
    return jax.ShapeDtypeStruct(shape, jnp.float32)


def after(rows):
    return pltpu.roll(rows, rows.shape[0] - 1, 0)


def before(rows):
    return pltpu.roll(rows, 1, 0)


def lift_rows(line, target, at, forward, place):
    cells = 128
    pairs = cells // 2
    wide = pairs + 8
    s = line[pl.ds(MARGIN + at - 8, wide, stride=2), :]
    d = line[pl.ds(MARGIN + at - 7, wide, stride=2), :]
    if forward:
        d = d + A * (s + after(s))
        s = s + B * (before(d) + d)
        d = d + C * (s + after(s))
        s = s + E * (before(d) + d)
        s = s * (1.0 / BALANCE)
        d = d * BALANCE
    else:
        s = s * BALANCE
        d = d * (1.0 / BALANCE)
        s = s - E * (before(d) + d)
        d = d - C * (s + after(s))
        s = s - B * (before(d) + d)
        d = d - A * (s + after(s))
    block = target.shape[0] // len(place)
    half = block // 2
    for k in range(cells // block):
        to = place[at // block + k] * block
        target[pl.ds(to, half, stride=2), :] = s[4 + k * half : 4 + (k + 1) * half]
        target[pl.ds(to + 1, half, stride=2), :] = d[4 + k * half : 4 + (k + 1) * half]


def mirror_start(line):
    for k in range(1, 9):
        line[pl.ds(MARGIN - k, 1), :] = line[pl.ds(MARGIN + k, 1), :]


def mirror_end(line, ny):
    for k in range(1, 9):
        line[pl.ds(MARGIN + ny - 1 + k, 1), :] = line[pl.ds(MARGIN + ny - 1 - k, 1), :]


def analyse_kernel(order, source, target, line, arrived):
    ny = source.shape[0]
    n = ny // CHUNK
    copies = []
    for k in range(n):
        inner = pl.ds(MARGIN + k * CHUNK, CHUNK)
        rows = pl.ds(k * CHUNK, CHUNK)
        copies.append(pltpu.make_async_copy(source.at[rows], line.at[inner], arrived.at[k]))
        copies[k].start()
    copies[0].wait()
    mirror_start(line)
    for k in range(n):
        if k + 1 < n:
            copies[k + 1].wait()
        else:
            mirror_end(line, ny)
        for at in range(k * CHUNK, (k + 1) * CHUNK, 128):
            lift_rows(line, target, at, True, places(order))


def analyse_columns(order, values):
    ny = values.shape[0]
    values = pltpu.with_memory_space_constraint(values, pltpu.HBM)
    scratch = [
        pltpu.VMEM((ny + 2 * MARGIN, X), jnp.float32),
        pltpu.SemaphoreType.DMA((ny // CHUNK,)),
    ]
    out_shape = pltpu.VMEM((ny, X), jnp.float32)
    kernel = functools.partial(analyse_kernel, order)
    return call(kernel, out_shape, [pltpu.HBM], scratch, "analyse_y")(values)


def synthesise_kernel(order, source, target, line, lifted, left):
    ny = source.shape[0]
    n = ny // CHUNK
    block = ny // len(order)
    for k, device in enumerate(order):
        line[pl.ds(MARGIN + device * block, block), :] = source[pl.ds(k * block, block), :]
    mirror_start(line)
    mirror_end(line, ny)
    copies = []
    for k in range(n):
        for at in range(k * CHUNK, (k + 1) * CHUNK, 128):
            lift_rows(line, lifted, at, False, range(len(order)))
        rows = pl.ds(k * CHUNK, CHUNK)
        copies.append(pltpu.make_async_copy(lifted.at[rows], target.at[rows], left.at[k]))
        copies[k].start()
    for copy in copies:
        copy.wait()


def synthesise_columns(order, values):
    ny = values.shape[0]
    scratch = [
        pltpu.VMEM((ny + 2 * MARGIN, X), jnp.float32),
        pltpu.VMEM((ny, X), jnp.float32),
        pltpu.SemaphoreType.DMA((ny // CHUNK,)),
    ]
    kernel = functools.partial(synthesise_kernel, order)
    return call(kernel, array(ny, X), [pltpu.VMEM], scratch, "synthesise_y", pltpu.HBM)(values)


def edge_kernel(values, to_left, to_right, edges):
    cells = values.shape[0]
    for at in range(0, cells, X):
        turned = values[pl.ds(at, X), :].T
        edges[0:EDGE, pl.ds(at, X)] = turned[:EDGE]
        edges[EDGE : 2 * EDGE, pl.ds(at, X)] = turned[X - EDGE :]

    def cell(k):
        return edges[pl.ds(k, 1), :]

    s = [cell(2 * n) for n in range(EDGE)]
    d = [cell(2 * n + 1) for n in range(EDGE)]
    d1 = {n: d[n] + A * (s[n] + s[n + 1]) for n in (0, 1, 2, 5, 6)}
    s1 = {n: s[n] + B * (d1[n - 1] + d1[n]) for n in (1, 2, 6)}
    to_left[0:1] = s[0]
    to_left[1:2] = d1[0]
    to_left[2:3] = s1[1]
    to_left[3:4] = d1[1] + C * (s1[1] + s1[2])
    to_right[0:1] = d[7] + A * s[7]
    to_right[1:2] = s[7] + B * d1[6]
    to_right[2:3] = d1[6] + C * s1[6]
    to_right[3:4] = jnp.zeros_like(s[0])


def edges_of(values):
    cells = values.shape[0]
    shapes = (array(4, cells), array(4, cells), array(2 * EDGE, cells))
    return call(edge_kernel, shapes, [pltpu.VMEM], name="edges_x")(values)


def analyse_depth(cells):
    n = len(cells) // 2
    s, d = cells[0::2], cells[1::2]

    def right(k):
        return s[min(k + 1, n - 1)]

    def left(k):
        return d[max(k - 1, 0)]

    d = [d[k] + A * (s[k] + right(k)) for k in range(n)]
    s = [s[k] + B * (left(k) + d[k]) for k in range(n)]
    d = [d[k] + C * (s[k] + right(k)) for k in range(n)]
    s = [s[k] + E * (left(k) + d[k]) for k in range(n)]
    return s, d


def synthesise_depth(s, d):
    n = len(s)

    def right(k):
        return s[min(k + 1, n - 1)]

    def left(k):
        return d[max(k - 1, 0)]

    s = [s[k] - E * (left(k) + d[k]) for k in range(n)]
    d = [d[k] - C * (s[k] + right(k)) for k in range(n)]
    s = [s[k] - B * (left(k) + d[k]) for k in range(n)]
    d = [d[k] - A * (s[k] + right(k)) for k in range(n)]
    return [v for pair in zip(s, d) for v in pair]


def gain_tables(gains, y_odd, x_odd):
    tables = []
    for z in range(2):
        low = jnp.where(x_odd, gains[z, 0, 1], gains[z, 0, 0])
        high = jnp.where(x_odd, gains[z, 1, 1], gains[z, 1, 0])
        tables.append(jnp.where(y_odd, high, low))
    return tables


def scale_tables(x_odd):
    along = jnp.where(x_odd, BALANCE, 1.0 / BALANCE)
    return along * (1.0 / BALANCE), along * BALANCE


def dot(left, right):
    return jnp.dot(left, right, precision=lax.Precision.HIGHEST, preferred_element_type=jnp.float32)


def split(values):
    first = values.astype(jnp.bfloat16)
    rest = values - first.astype(jnp.float32)
    second = rest.astype(jnp.bfloat16)
    third = (rest - second.astype(jnp.float32)).astype(jnp.bfloat16)
    return first, second, third


def split_matrix(matrix):
    matrix = np.asarray(matrix, np.float32)
    first = matrix.astype(jnp.bfloat16)
    rest = matrix - first.astype(np.float32)
    second = rest.astype(jnp.bfloat16)
    third = (rest - second.astype(np.float32)).astype(jnp.bfloat16)
    wide = np.concatenate([np.concatenate([first, second], 1)] * 2, 0)
    return jnp.asarray(wide), jnp.asarray(np.concatenate([third, first], 0))


def split_dot(values, wide, tall):
    first, second, third = split(values)
    large = jnp.dot(jnp.concatenate([first, second], 1), wide, preferred_element_type=jnp.float32)
    small = jnp.dot(jnp.concatenate([first, third], 1), tall, preferred_element_type=jnp.float32)
    return large[:, :X] + (large[:, X:] + small)


def main_kernel(
    order, values, gains, edges, forward, forward_tall, backward, backward_tall, coefficients, rebuilt
):
    del edges
    nz, ny, _ = values.shape
    place = places(order)
    lane = lax.broadcasted_iota(jnp.int32, (ROWS, X), 1)
    row = lax.broadcasted_iota(jnp.int32, (ROWS, X), 0)
    gain_low, gain_high = gain_tables(gains, row % 2 == 1, lane % 2 == 1)
    scale_low, scale_high = scale_tables(lane % 2 == 1)
    lines = split_dot(values[...].reshape(nz * ny, X), forward[...], forward_tall[...])
    rebuilt[...] = lines.reshape(nz, ny, X)

    def body(k, carry):
        rows = pl.ds(pl.multiple_of(k * ROWS, ROWS), ROWS)
        s, d = analyse_depth([rebuilt[place[z], rows, :] for z in range(nz)])
        for n in range(nz // 2):
            coefficients[2 * n, rows, :] = s[n] * scale_low
            coefficients[2 * n + 1, rows, :] = d[n] * scale_high
        cells = synthesise_depth([v * gain_low for v in s], [v * gain_high for v in d])
        for z in range(nz):
            rebuilt[place[z], rows, :] = cells[z]
        return carry

    lax.fori_loop(0, ny // ROWS, body, 0)
    lines = split_dot(rebuilt[...].reshape(nz * ny, X), backward[...], backward_tall[...])
    rebuilt[...] = lines.reshape(nz, ny, X)


def main_depths(order, values, gains, edges):
    shape = array(*values.shape)
    size = values.size
    cost = pl.CostEstimate(flops=100 * size, bytes_accessed=12 * size, transcendentals=0)
    spaces = [pltpu.VMEM, pltpu.SMEM, pl.ANY] + [pltpu.VMEM] * 4
    forward = split_matrix(own_analysis_matrix())
    backward = split_matrix(synthesis_matrix()[:, :X].T)
    kernel = functools.partial(main_kernel, order)
    return call(kernel, (shape, shape), spaces, name="depth_main", cost=cost)(
        values, gains, edges, *forward, *backward
    )


def halo_kernel(
    blocks, order, own_coefficients, own_rebuilt, from_right, from_left, edges, gains, weights, spread,
    coefficients, rebuilt, held, left,
):
    nz = own_rebuilt.shape[0]
    index = lax.axis_index("ba")
    kind = 2 * (index == 0).astype(jnp.int32) + (index == blocks - 1).astype(jnp.int32)
    halo = jnp.concatenate([from_right[...], from_left[...], edges[...]], 0)
    found = dot(weights[kind], halo)
    lane = lax.broadcasted_iota(jnp.int32, (ROWS, X), 1)
    row = lax.broadcasted_iota(jnp.int32, (ROWS, X), 0)
    low = lane < HALF
    low_16 = lax.broadcasted_iota(jnp.int32, (16, X), 1) < HALF
    cells = []
    for k in range(nz // 2):
        inside = found[0:8, k * X : (k + 1) * X]
        beyond = found[8:16, k * X : (k + 1) * X]
        cells.append(jnp.where(low, inside, pltpu.roll(beyond, HALF, 1)))
        cells.append(jnp.where(low, pltpu.roll(inside, HALF, 1), beyond))
    x_odd = (row + jnp.where(low | (row < 4), 0, 1)) % 2 == 1
    gain_low, gain_high = gain_tables(gains, lane % 2 == 1, x_odd)
    scale_low, scale_high = scale_tables(x_odd)
    s, d = analyse_depth([cells[k] for k in places(order)])
    middle = jnp.zeros((X - 16, X), jnp.float32)
    copies = []
    for k in range(nz // 2):
        both = jnp.where(low, s[k] * scale_low, pltpu.roll(d[k] * scale_high, HALF, 1))
        ends = [jnp.where(row < 4, both, 0.0), middle, jnp.where(row < 4, 0.0, both)]
        turned = jnp.concatenate(ends, 0).T
        held[2 * k] = own_coefficients[2 * k] + turned[:HALF]
        held[2 * k + 1] = own_coefficients[2 * k + 1] + turned[HALF:]
        if k % 2 == 1:
            part = pl.ds(2 * k - 2, 4)
            copies.append(pltpu.make_async_copy(held.at[part], coefficients.at[part], left.at[k // 2]))
            copies[-1].start()
    cells = synthesise_depth([v * gain_low for v in s], [v * gain_high for v in d])
    table = [spread[:, k * X : (k + 1) * X] for k in range(8)]
    for k in range(nz // 2):
        mixed = []
        for v in (cells[order[2 * k]], cells[order[2 * k + 1]]):
            total = None
            for m in range(8):
                term = table[m] * jnp.broadcast_to(v[m : m + 1], (16, X))
                total = term if total is None else total + term
            mixed.append(total + pltpu.roll(total, HALF, 1))
        both = jnp.where(low_16, *mixed)
        turned = jnp.concatenate([both[:8], middle, both[8:]], 0).T
        rebuilt[2 * k] = own_rebuilt[2 * k] + turned[:HALF]
        rebuilt[2 * k + 1] = own_rebuilt[2 * k + 1] + turned[HALF:]
    for copy in copies:
        copy.wait()


def add_halo(blocks, order, own_coefficients, own_rebuilt, from_right, from_left, edges, gains):
    shape = own_rebuilt.shape
    nz = shape[0]
    kinds = [correction_matrix(left, right) for left in (False, True) for right in (False, True)]
    mixing = edge_synthesis_matrix()
    spread = np.zeros((16, 8, X))
    spread[:, :, :HALF] = mixing[:, :8, None]
    spread[:, :, HALF:] = mixing[:, 8:, None]
    spaces = [pltpu.VMEM] * 5 + [pltpu.SMEM] + [pltpu.VMEM] * 2
    scratch = [pltpu.VMEM(shape, jnp.float32), pltpu.SemaphoreType.DMA((nz // 4,))]
    kernel = functools.partial(halo_kernel, blocks, order)
    out_space = (pltpu.HBM, pltpu.VMEM)
    return call(kernel, (array(*shape), array(*shape)), spaces, scratch, "depth_halo", out_space)(
        own_coefficients, own_rebuilt, from_right, from_left, edges, gains,
        jnp.asarray(np.stack(kinds), jnp.float32), jnp.asarray(spread.reshape(16, 8 * X), jnp.float32),
    )


def per_device(blocks, field, gains):
    nz = lax.axis_size("aa")
    ny = field.shape[1]
    order = exchange_order(nz)

    def exchange(blocks_):
        blocks_ = blocks_.reshape(nz, ny // nz, X)
        return lax.all_to_all(blocks_, "aa", 0, 0, axis_index_groups=[order], tiled=True)

    by_depth = exchange(analyse_columns(order, field.reshape(ny, X)))
    to_left, to_right, edges = edges_of(by_depth.reshape(ny, X))
    from_right = lax.ppermute(to_left, "ba", [(k, k - 1) for k in range(1, blocks)])
    from_left = lax.ppermute(to_right, "ba", [(k, k + 1) for k in range(blocks - 1)])
    own_coefficients, own_rebuilt = main_depths(order, by_depth, gains, edges)
    coefficients, rebuilt = add_halo(
        blocks, order, own_coefficients, own_rebuilt, from_right, from_left, edges, gains
    )
    rebuilt = synthesise_columns(order, exchange(rebuilt).reshape(ny, X))
    return coefficients, rebuilt.reshape(1, ny, X)


def solution(mesh):
    return jax.shard_map(
        functools.partial(per_device, mesh.shape["ba"]),
        mesh=mesh,
        in_specs=(P("aa", None, "ba"), P()),
        out_specs=(P(None, "aa", "ba"), P("aa", None, "ba")),
        check_vma=False,
    )
```

```python
import functools

import jax
import jax.numpy as jnp
import numpy as np
from jax import lax
from jax.experimental import pallas as pl
from jax.experimental.pallas import tpu as pltpu
from jax.sharding import PartitionSpec as P

PREDICT_FIRST = -1.586134342059924
UPDATE_FIRST = -0.052980118572961
PREDICT_SECOND = 0.882911075530934
UPDATE_SECOND = 0.443506852043971
BALANCE = 1.230174104914001
A, B, C, E = PREDICT_FIRST, UPDATE_FIRST, PREDICT_SECOND, UPDATE_SECOND

X = 128
HALF = X // 2
ROWS = 8
MARGIN = 16
CHUNK = 256
VMEM_LIMIT = 24 * 1024 * 1024
EDGE = 8
HIGHEST = lax.Precision.HIGHEST

def exchange_order(n):
    if n != 32:
        return [(k + 2) % n for k in range(n)]

    def where(k):
        return k // 8, k // 2 % 4, k % 2

    first = 11

    def distance(k):
        (x, y, core), (x_first, y_first, core_first) = where(k), where(first)
        along = abs(x - x_first)
        return 10 * (min(along, 4 - along) + abs(y - y_first)) + (core != core_first)

    rest = [k for k in range(n) if k != first]
    return [first, *sorted(rest, key=lambda k: -distance(k))]


def places(order):
    out = [0] * len(order)
    for k, device in enumerate(order):
        out[device] = k
    return out


def edge_matrix():
    unit = np.eye(X)
    s, d = unit[0::2], unit[1::2]
    d1 = [d[n] + A * (s[n] + s[n + 1]) for n in range(HALF - 1)]
    s1 = [None] + [s[n] + B * (d1[n - 1] + d1[n]) for n in range(1, HALF - 1)]
    last = HALF - 1
    out = np.zeros((16, X))
    out[0] = s[0]
    out[1] = d1[0]
    out[2] = s1[1]
    out[3] = d1[1] + C * (s1[1] + s1[2])
    out[4] = d[last] + A * s[last]
    out[5] = s[last] + B * d1[last - 1]
    out[6] = d1[last - 1] + C * s1[last - 1]
    out[8] = d[0] + A * s[1]
    out[9] = s[1] + B * d1[1]
    out[10] = d1[1] + C * s1[2]
    out[12] = s[last]
    out[13] = d1[last - 1]
    out[14] = s1[last - 1]
    out[15] = d1[last - 2] + C * (s1[last - 2] + s1[last - 1])
    return np.concatenate([out[:, :EDGE], out[:, X - EDGE :]], 1)


def correction_matrix(left_end, right_end):
    unit = np.eye(24)
    own = unit[8:]
    h0, h1, h2, h3 = own[12:16] if right_end else unit[0:4]
    hp, hq, hr = own[8:11] if left_end else unit[4:7]
    s0, d10, p, q = own[0], own[1], own[4], own[5]
    add_d1 = A * h0
    d1 = p + add_d1
    s1_next = h0 + B * (d1 + h1)
    add_s1 = B * add_d1
    add_d2 = add_d1 + C * (add_s1 + s1_next)
    add_d2_before = C * add_s1
    add_s2 = add_s1 + E * (add_d2_before + add_d2)
    add_s2_before = E * add_d2_before
    s1 = q + B * d1
    d2 = d1 + C * (s1 + s1_next)
    d2_next = h1 + C * (s1_next + h2)
    s2_next = s1_next + E * (d2 + d2_next)
    s2_after = h2 + E * (d2_next + h3)
    right = [add_s2_before, add_d2_before, add_s2, add_d2]
    right_beyond = [s2_next, d2_next, s2_after, h3]
    d1_out = hp + A * s0
    s1_out = hq + B * d1_out
    add_s1 = B * d1_out
    s1 = s0 + B * (d1_out + d10)
    add_d2 = C * add_s1
    d2_out = d1_out + C * (s1_out + s1)
    d2_far = hr + C * s1_out
    s2_out = s1_out + E * (d2_far + d2_out)
    left = [add_s1 + E * (d2_out + add_d2), add_d2, E * add_d2, 0 * s0]
    left_beyond = [d2_out, s2_out, d2_far, 0 * s0]
    found = np.stack(left + right + right_beyond + left_beyond)
    return np.concatenate([found[:, :8], found[:, 8:] @ edge_matrix()], 1)


def own_analysis_matrix():
    unit = np.eye(X)
    zero = np.zeros((1, X))
    s, d = unit[0::2], unit[1::2]
    d = d + A * (s + np.concatenate([s[1:], zero]))
    s = s + B * (d + np.concatenate([zero, d[:-1]]))
    d = d + C * (s + np.concatenate([s[1:], zero]))
    s = s + E * (d + np.concatenate([zero, d[:-1]]))
    out = np.zeros((X, X))
    out[:, 0::2] = s.T
    out[:, 1::2] = d.T
    return out


def synthesis_matrix():
    unit = np.eye(X + 8)
    place = {k: k for k in range(X + 4)}
    place.update({-1: X + 4, -2: X + 5, -3: X + 6})
    n_all = HALF
    s2 = {n: unit[place[2 * n]] for n in range(-1, n_all + 2)}
    d2 = {n: unit[place[2 * n + 1]] for n in range(-2, n_all + 2)}
    s1 = {n: s2[n] - E * (d2[n - 1] + d2[n]) for n in range(-1, n_all + 2)}
    d1 = {n: d2[n] - C * (s1[n] + s1[n + 1]) for n in range(-1, n_all + 1)}
    s = {n: s1[n] - B * (d1[n - 1] + d1[n]) for n in range(n_all + 1)}
    d = {n: d1[n] - A * (s[n] + s[n + 1]) for n in range(n_all)}
    cells = np.zeros((X, X + 8))
    cells[0::2] = [s[n] for n in range(n_all)]
    cells[1::2] = [d[n] for n in range(n_all)]
    return cells


def edge_synthesis_matrix():
    inside = [0, 1, 2, 3, 124, 125, 126, 127] + [X + k for k in range(8)]
    return synthesis_matrix()[list(range(8)) + list(range(120, 128))][:, inside]


def call(kernel, out_shape, spaces, scratch=(), name=None, out_space=pltpu.VMEM, cost=None):
    if isinstance(out_space, tuple):
        out_specs = tuple(pl.BlockSpec(memory_space=space) for space in out_space)
    else:
        out_specs = jax.tree.map(lambda _: pl.BlockSpec(memory_space=out_space), out_shape)
    return pl.pallas_call(
        kernel,
        out_shape=out_shape,
        in_specs=[pl.BlockSpec(memory_space=space) for space in spaces],
        out_specs=out_specs,
        scratch_shapes=list(scratch),
        compiler_params=pltpu.CompilerParams(vmem_limit_bytes=VMEM_LIMIT),
        cost_estimate=cost,
        name=name,
    )


def array(*shape):
    return jax.ShapeDtypeStruct(shape, jnp.float32)


def after(rows):
    return pltpu.roll(rows, rows.shape[0] - 1, 0)


def before(rows):
    return pltpu.roll(rows, 1, 0)


def lift_rows(line, target, at, forward, place):
    cells = 128
    pairs = cells // 2
    wide = pairs + 8
    s = line[pl.ds(MARGIN + at - 8, wide, stride=2), :]
    d = line[pl.ds(MARGIN + at - 7, wide, stride=2), :]
    if forward:
        d = d + A * (s + after(s))
        s = s + B * (before(d) + d)
        d = d + C * (s + after(s))
        s = s + E * (before(d) + d)
        s = s * (1.0 / BALANCE)
        d = d * BALANCE
    else:
        s = s * BALANCE
        d = d * (1.0 / BALANCE)
        s = s - E * (before(d) + d)
        d = d - C * (s + after(s))
        s = s - B * (before(d) + d)
        d = d - A * (s + after(s))
    block = target.shape[0] // len(place)
    half = block // 2
    for k in range(cells // block):
        to = place[at // block + k] * block
        target[pl.ds(to, half, stride=2), :] = s[4 + k * half : 4 + (k + 1) * half]
        target[pl.ds(to + 1, half, stride=2), :] = d[4 + k * half : 4 + (k + 1) * half]


def mirror_start(line):
    for k in range(1, 9):
        line[pl.ds(MARGIN - k, 1), :] = line[pl.ds(MARGIN + k, 1), :]


def mirror_end(line, ny):
    for k in range(1, 9):
        line[pl.ds(MARGIN + ny - 1 + k, 1), :] = line[pl.ds(MARGIN + ny - 1 - k, 1), :]


def analyse_kernel(order, source, target, line, arrived):
    ny = source.shape[0]
    n = ny // CHUNK
    copies = []
    for k in range(n):
        inner = pl.ds(MARGIN + k * CHUNK, CHUNK)
        rows = pl.ds(k * CHUNK, CHUNK)
        copies.append(pltpu.make_async_copy(source.at[rows], line.at[inner], arrived.at[k]))
        copies[k].start()
    copies[0].wait()
    mirror_start(line)
    for k in range(n):
        if k + 1 < n:
            copies[k + 1].wait()
        else:
            mirror_end(line, ny)
        for at in range(k * CHUNK, (k + 1) * CHUNK, 128):
            lift_rows(line, target, at, True, places(order))


def analyse_columns(order, values):
    ny = values.shape[0]
    values = pltpu.with_memory_space_constraint(values, pltpu.HBM)
    scratch = [
        pltpu.VMEM((ny + 2 * MARGIN, X), jnp.float32),
        pltpu.SemaphoreType.DMA((ny // CHUNK,)),
    ]
    out_shape = pltpu.VMEM((ny, X), jnp.float32)
    kernel = functools.partial(analyse_kernel, order)
    return call(kernel, out_shape, [pltpu.HBM], scratch, "analyse_y")(values)


def synthesise_kernel(order, source, target, line, lifted, left):
    ny = source.shape[0]
    n = ny // CHUNK
    block = ny // len(order)
    for k, device in enumerate(order):
        line[pl.ds(MARGIN + device * block, block), :] = source[pl.ds(k * block, block), :]
    mirror_start(line)
    mirror_end(line, ny)
    copies = []
    for k in range(n):
        for at in range(k * CHUNK, (k + 1) * CHUNK, 128):
            lift_rows(line, lifted, at, False, range(len(order)))
        rows = pl.ds(k * CHUNK, CHUNK)
        copies.append(pltpu.make_async_copy(lifted.at[rows], target.at[rows], left.at[k]))
        copies[k].start()
    for copy in copies:
        copy.wait()


def synthesise_columns(order, values):
    ny = values.shape[0]
    scratch = [
        pltpu.VMEM((ny + 2 * MARGIN, X), jnp.float32),
        pltpu.VMEM((ny, X), jnp.float32),
        pltpu.SemaphoreType.DMA((ny // CHUNK,)),
    ]
    kernel = functools.partial(synthesise_kernel, order)
    return call(kernel, array(ny, X), [pltpu.VMEM], scratch, "synthesise_y", pltpu.HBM)(values)


def edge_kernel(values, to_left, to_right, edges):
    cells = values.shape[0]
    for at in range(0, cells, X):
        turned = values[pl.ds(at, X), :].T
        edges[0:EDGE, pl.ds(at, X)] = turned[:EDGE]
        edges[EDGE : 2 * EDGE, pl.ds(at, X)] = turned[X - EDGE :]

    def cell(k):
        return edges[pl.ds(k, 1), :]

    s = [cell(2 * n) for n in range(EDGE)]
    d = [cell(2 * n + 1) for n in range(EDGE)]
    d1 = {n: d[n] + A * (s[n] + s[n + 1]) for n in (0, 1, 2, 5, 6)}
    s1 = {n: s[n] + B * (d1[n - 1] + d1[n]) for n in (1, 2, 6)}
    to_left[0:1] = s[0]
    to_left[1:2] = d1[0]
    to_left[2:3] = s1[1]
    to_left[3:4] = d1[1] + C * (s1[1] + s1[2])
    to_right[0:1] = d[7] + A * s[7]
    to_right[1:2] = s[7] + B * d1[6]
    to_right[2:3] = d1[6] + C * s1[6]
    to_right[3:4] = jnp.zeros_like(s[0])


def edges_of(values):
    cells = values.shape[0]
    shapes = (array(4, cells), array(4, cells), array(2 * EDGE, cells))
    return call(edge_kernel, shapes, [pltpu.VMEM], name="edges_x")(values)


def analyse_depth(cells):
    n = len(cells) // 2
    s, d = cells[0::2], cells[1::2]

    def right(k):
        return s[min(k + 1, n - 1)]

    def left(k):
        return d[max(k - 1, 0)]

    d = [d[k] + A * (s[k] + right(k)) for k in range(n)]
    s = [s[k] + B * (left(k) + d[k]) for k in range(n)]
    d = [d[k] + C * (s[k] + right(k)) for k in range(n)]
    s = [s[k] + E * (left(k) + d[k]) for k in range(n)]
    return s, d


def synthesise_depth(s, d):
    n = len(s)

    def right(k):
        return s[min(k + 1, n - 1)]

    def left(k):
        return d[max(k - 1, 0)]

    s = [s[k] - E * (left(k) + d[k]) for k in range(n)]
    d = [d[k] - C * (s[k] + right(k)) for k in range(n)]
    s = [s[k] - B * (left(k) + d[k]) for k in range(n)]
    d = [d[k] - A * (s[k] + right(k)) for k in range(n)]
    return [v for pair in zip(s, d) for v in pair]


def gain_tables(gains, y_odd, x_odd):
    tables = []
    for z in range(2):
        low = jnp.where(x_odd, gains[z, 0, 1], gains[z, 0, 0])
        high = jnp.where(x_odd, gains[z, 1, 1], gains[z, 1, 0])
        tables.append(jnp.where(y_odd, high, low))
    return tables


def scale_tables(x_odd):
    along = jnp.where(x_odd, BALANCE, 1.0 / BALANCE)
    return along * (1.0 / BALANCE), along * BALANCE


def dot(left, right):
    return jnp.dot(left, right, precision=lax.Precision.HIGHEST, preferred_element_type=jnp.float32)


def split(values):
    first = values.astype(jnp.bfloat16)
    rest = values - first.astype(jnp.float32)
    second = rest.astype(jnp.bfloat16)
    third = (rest - second.astype(jnp.float32)).astype(jnp.bfloat16)
    return first, second, third


def split_matrix(matrix):
    matrix = np.asarray(matrix, np.float32)
    first = matrix.astype(jnp.bfloat16)
    rest = matrix - first.astype(np.float32)
    second = rest.astype(jnp.bfloat16)
    third = (rest - second.astype(np.float32)).astype(jnp.bfloat16)
    wide = np.concatenate([np.concatenate([first, second], 1)] * 2, 0)
    return jnp.asarray(wide), jnp.asarray(np.concatenate([third, first], 0))


def split_dot(values, wide, tall):
    first, second, third = split(values)
    large = jnp.dot(jnp.concatenate([first, second], 1), wide, preferred_element_type=jnp.float32)
    small = jnp.dot(jnp.concatenate([first, third], 1), tall, preferred_element_type=jnp.float32)
    return large[:, :X] + (large[:, X:] + small)


def main_kernel(
    order, values, gains, edges, forward, forward_tall, backward, backward_tall, coefficients, rebuilt
):
    del edges
    nz, ny, _ = values.shape
    place = places(order)
    lane = lax.broadcasted_iota(jnp.int32, (ROWS, X), 1)
    row = lax.broadcasted_iota(jnp.int32, (ROWS, X), 0)
    gain_low, gain_high = gain_tables(gains, row % 2 == 1, lane % 2 == 1)
    scale_low, scale_high = scale_tables(lane % 2 == 1)
    lines = split_dot(values[...].reshape(nz * ny, X), forward[...], forward_tall[...])
    rebuilt[...] = lines.reshape(nz, ny, X)

    def body(k, carry):
        rows = pl.ds(pl.multiple_of(k * ROWS, ROWS), ROWS)
        s, d = analyse_depth([rebuilt[place[z], rows, :] for z in range(nz)])
        for n in range(nz // 2):
            coefficients[2 * n, rows, :] = s[n] * scale_low
            coefficients[2 * n + 1, rows, :] = d[n] * scale_high
        cells = synthesise_depth([v * gain_low for v in s], [v * gain_high for v in d])
        for z in range(nz):
            rebuilt[place[z], rows, :] = cells[z]
        return carry

    lax.fori_loop(0, ny // ROWS, body, 0)
    lines = split_dot(rebuilt[...].reshape(nz * ny, X), backward[...], backward_tall[...])
    rebuilt[...] = lines.reshape(nz, ny, X)


def main_depths(order, values, gains, edges):
    shape = array(*values.shape)
    size = values.size
    cost = pl.CostEstimate(flops=100 * size, bytes_accessed=12 * size, transcendentals=0)
    spaces = [pltpu.VMEM, pltpu.SMEM, pl.ANY] + [pltpu.VMEM] * 4
    forward = split_matrix(own_analysis_matrix())
    backward = split_matrix(synthesis_matrix()[:, :X].T)
    kernel = functools.partial(main_kernel, order)
    return call(kernel, (shape, shape), spaces, name="depth_main", cost=cost)(
        values, gains, edges, *forward, *backward
    )


def halo_kernel(
    blocks, order, own_coefficients, own_rebuilt, from_right, from_left, edges, gains, weights, spread,
    coefficients, rebuilt, held, left,
):
    nz = own_rebuilt.shape[0]
    index = lax.axis_index("ba")
    kind = 2 * (index == 0).astype(jnp.int32) + (index == blocks - 1).astype(jnp.int32)
    halo = jnp.concatenate([from_right[...], from_left[...], edges[...]], 0)
    found = dot(weights[kind], halo)
    lane = lax.broadcasted_iota(jnp.int32, (ROWS, X), 1)
    row = lax.broadcasted_iota(jnp.int32, (ROWS, X), 0)
    low = lane < HALF
    low_16 = lax.broadcasted_iota(jnp.int32, (16, X), 1) < HALF
    cells = []
    for k in range(nz // 2):
        inside = found[0:8, k * X : (k + 1) * X]
        beyond = found[8:16, k * X : (k + 1) * X]
        cells.append(jnp.where(low, inside, pltpu.roll(beyond, HALF, 1)))
        cells.append(jnp.where(low, pltpu.roll(inside, HALF, 1), beyond))
    x_odd = (row + jnp.where(low | (row < 4), 0, 1)) % 2 == 1
    gain_low, gain_high = gain_tables(gains, lane % 2 == 1, x_odd)
    scale_low, scale_high = scale_tables(x_odd)
    s, d = analyse_depth([cells[k] for k in places(order)])
    middle = jnp.zeros((X - 16, X), jnp.float32)
    copies = []
    for k in range(nz // 2):
        both = jnp.where(low, s[k] * scale_low, pltpu.roll(d[k] * scale_high, HALF, 1))
        ends = [jnp.where(row < 4, both, 0.0), middle, jnp.where(row < 4, 0.0, both)]
        turned = jnp.concatenate(ends, 0).T
        held[2 * k] = own_coefficients[2 * k] + turned[:HALF]
        held[2 * k + 1] = own_coefficients[2 * k + 1] + turned[HALF:]
        if k % 2 == 1:
            part = pl.ds(2 * k - 2, 4)
            copies.append(pltpu.make_async_copy(held.at[part], coefficients.at[part], left.at[k // 2]))
            copies[-1].start()
    cells = synthesise_depth([v * gain_low for v in s], [v * gain_high for v in d])
    table = [spread[:, k * X : (k + 1) * X] for k in range(8)]
    for k in range(nz // 2):
        mixed = []
        for v in (cells[order[2 * k]], cells[order[2 * k + 1]]):
            total = None
            for m in range(8):
                term = table[m] * jnp.broadcast_to(v[m : m + 1], (16, X))
                total = term if total is None else total + term
            mixed.append(total + pltpu.roll(total, HALF, 1))
        both = jnp.where(low_16, *mixed)
        turned = jnp.concatenate([both[:8], middle, both[8:]], 0).T
        rebuilt[2 * k] = own_rebuilt[2 * k] + turned[:HALF]
        rebuilt[2 * k + 1] = own_rebuilt[2 * k + 1] + turned[HALF:]
    for copy in copies:
        copy.wait()


def add_halo(blocks, order, own_coefficients, own_rebuilt, from_right, from_left, edges, gains):
    shape = own_rebuilt.shape
    nz = shape[0]
    kinds = [correction_matrix(left, right) for left in (False, True) for right in (False, True)]
    mixing = edge_synthesis_matrix()
    spread = np.zeros((16, 8, X))
    spread[:, :, :HALF] = mixing[:, :8, None]
    spread[:, :, HALF:] = mixing[:, 8:, None]
    spaces = [pltpu.VMEM] * 5 + [pltpu.SMEM] + [pltpu.VMEM] * 2
    scratch = [pltpu.VMEM(shape, jnp.float32), pltpu.SemaphoreType.DMA((nz // 4,))]
    kernel = functools.partial(halo_kernel, blocks, order)
    out_space = (pltpu.HBM, pltpu.VMEM)
    return call(kernel, (array(*shape), array(*shape)), spaces, scratch, "depth_halo", out_space)(
        own_coefficients, own_rebuilt, from_right, from_left, edges, gains,
        jnp.asarray(np.stack(kinds), jnp.float32), jnp.asarray(spread.reshape(16, 8 * X), jnp.float32),
    )


def per_device(blocks, field, gains):
    nz = lax.axis_size("aa")
    ny = field.shape[1]
    order = exchange_order(nz)

    def exchange(blocks_):
        blocks_ = blocks_.reshape(nz, ny // nz, X)
        return lax.all_to_all(blocks_, "aa", 0, 0, axis_index_groups=[order], tiled=True)

    by_depth = exchange(analyse_columns(order, field.reshape(ny, X)))
    to_left, to_right, edges = edges_of(by_depth.reshape(ny, X))
    from_right = lax.ppermute(to_left, "ba", [(k, k - 1) for k in range(1, blocks)])
    from_left = lax.ppermute(to_right, "ba", [(k, k + 1) for k in range(blocks - 1)])
    own_coefficients, own_rebuilt = main_depths(order, by_depth, gains, edges)
    coefficients, rebuilt = add_halo(
        blocks, order, own_coefficients, own_rebuilt, from_right, from_left, edges, gains
    )
    rebuilt = synthesise_columns(order, exchange(rebuilt).reshape(ny, X))
    return coefficients, rebuilt.reshape(1, ny, X)


def solution(mesh):
    return jax.shard_map(
        functools.partial(per_device, mesh.shape["ba"]),
        mesh=mesh,
        in_specs=(P("aa", None, "ba"), P()),
        out_specs=(P(None, "aa", "ba"), P("aa", None, "ba")),
        check_vma=False,
    )
```

```python
import functools

import jax
import jax.numpy as jnp
import numpy as np
from jax import lax
from jax.experimental import pallas as pl
from jax.experimental.pallas import tpu as pltpu
from jax.sharding import PartitionSpec as P

PREDICT_FIRST = -1.586134342059924
UPDATE_FIRST = -0.052980118572961
PREDICT_SECOND = 0.882911075530934
UPDATE_SECOND = 0.443506852043971
BALANCE = 1.230174104914001
A, B, C, E = PREDICT_FIRST, UPDATE_FIRST, PREDICT_SECOND, UPDATE_SECOND

X = 128
HALF = X // 2
ROWS = 8
MARGIN = 16
CHUNK = 256
VMEM_LIMIT = 24 * 1024 * 1024
EDGE = 8
HIGHEST = lax.Precision.HIGHEST

def exchange_order(n):
    if n != 32:
        return [(k + 2) % n for k in range(n)]

    def where(k):
        return k // 8, k // 2 % 4, k % 2

    first = 11

    def distance(k):
        (x, y, core), (x_first, y_first, core_first) = where(k), where(first)
        along = abs(x - x_first)
        return 10 * (min(along, 4 - along) + abs(y - y_first)) + (core != core_first)

    rest = [k for k in range(n) if k != first]
    return [first, *sorted(rest, key=lambda k: -distance(k))]


def places(order):
    out = [0] * len(order)
    for k, device in enumerate(order):
        out[device] = k
    return out


def edge_matrix():
    unit = np.eye(X)
    s, d = unit[0::2], unit[1::2]
    d1 = [d[n] + A * (s[n] + s[n + 1]) for n in range(HALF - 1)]
    s1 = [None] + [s[n] + B * (d1[n - 1] + d1[n]) for n in range(1, HALF - 1)]
    last = HALF - 1
    out = np.zeros((16, X))
    out[0] = s[0]
    out[1] = d1[0]
    out[2] = s1[1]
    out[3] = d1[1] + C * (s1[1] + s1[2])
    out[4] = d[last] + A * s[last]
    out[5] = s[last] + B * d1[last - 1]
    out[6] = d1[last - 1] + C * s1[last - 1]
    out[8] = d[0] + A * s[1]
    out[9] = s[1] + B * d1[1]
    out[10] = d1[1] + C * s1[2]
    out[12] = s[last]
    out[13] = d1[last - 1]
    out[14] = s1[last - 1]
    out[15] = d1[last - 2] + C * (s1[last - 2] + s1[last - 1])
    return np.concatenate([out[:, :EDGE], out[:, X - EDGE :]], 1)


def correction_matrix(left_end, right_end):
    unit = np.eye(24)
    own = unit[8:]
    h0, h1, h2, h3 = own[12:16] if right_end else unit[0:4]
    hp, hq, hr = own[8:11] if left_end else unit[4:7]
    s0, d10, p, q = own[0], own[1], own[4], own[5]
    add_d1 = A * h0
    d1 = p + add_d1
    s1_next = h0 + B * (d1 + h1)
    add_s1 = B * add_d1
    add_d2 = add_d1 + C * (add_s1 + s1_next)
    add_d2_before = C * add_s1
    add_s2 = add_s1 + E * (add_d2_before + add_d2)
    add_s2_before = E * add_d2_before
    s1 = q + B * d1
    d2 = d1 + C * (s1 + s1_next)
    d2_next = h1 + C * (s1_next + h2)
    s2_next = s1_next + E * (d2 + d2_next)
    s2_after = h2 + E * (d2_next + h3)
    right = [add_s2_before, add_d2_before, add_s2, add_d2]
    right_beyond = [s2_next, d2_next, s2_after, h3]
    d1_out = hp + A * s0
    s1_out = hq + B * d1_out
    add_s1 = B * d1_out
    s1 = s0 + B * (d1_out + d10)
    add_d2 = C * add_s1
    d2_out = d1_out + C * (s1_out + s1)
    d2_far = hr + C * s1_out
    s2_out = s1_out + E * (d2_far + d2_out)
    left = [add_s1 + E * (d2_out + add_d2), add_d2, E * add_d2, 0 * s0]
    left_beyond = [d2_out, s2_out, d2_far, 0 * s0]
    found = np.stack(left + right + right_beyond + left_beyond)
    return np.concatenate([found[:, :8], found[:, 8:] @ edge_matrix()], 1)


def own_analysis_matrix():
    unit = np.eye(X)
    zero = np.zeros((1, X))
    s, d = unit[0::2], unit[1::2]
    d = d + A * (s + np.concatenate([s[1:], zero]))
    s = s + B * (d + np.concatenate([zero, d[:-1]]))
    d = d + C * (s + np.concatenate([s[1:], zero]))
    s = s + E * (d + np.concatenate([zero, d[:-1]]))
    out = np.zeros((X, X))
    out[:, 0::2] = s.T
    out[:, 1::2] = d.T
    return out


def synthesis_matrix():
    unit = np.eye(X + 8)
    place = {k: k for k in range(X + 4)}
    place.update({-1: X + 4, -2: X + 5, -3: X + 6})
    n_all = HALF
    s2 = {n: unit[place[2 * n]] for n in range(-1, n_all + 2)}
    d2 = {n: unit[place[2 * n + 1]] for n in range(-2, n_all + 2)}
    s1 = {n: s2[n] - E * (d2[n - 1] + d2[n]) for n in range(-1, n_all + 2)}
    d1 = {n: d2[n] - C * (s1[n] + s1[n + 1]) for n in range(-1, n_all + 1)}
    s = {n: s1[n] - B * (d1[n - 1] + d1[n]) for n in range(n_all + 1)}
    d = {n: d1[n] - A * (s[n] + s[n + 1]) for n in range(n_all)}
    cells = np.zeros((X, X + 8))
    cells[0::2] = [s[n] for n in range(n_all)]
    cells[1::2] = [d[n] for n in range(n_all)]
    return cells


def edge_synthesis_matrix():
    inside = [0, 1, 2, 3, 124, 125, 126, 127] + [X + k for k in range(8)]
    return synthesis_matrix()[list(range(8)) + list(range(120, 128))][:, inside]


def call(kernel, out_shape, spaces, scratch=(), name=None, out_space=pltpu.VMEM, cost=None):
    if isinstance(out_space, tuple):
        out_specs = tuple(pl.BlockSpec(memory_space=space) for space in out_space)
    else:
        out_specs = jax.tree.map(lambda _: pl.BlockSpec(memory_space=out_space), out_shape)
    return pl.pallas_call(
        kernel,
        out_shape=out_shape,
        in_specs=[pl.BlockSpec(memory_space=space) for space in spaces],
        out_specs=out_specs,
        scratch_shapes=list(scratch),
        compiler_params=pltpu.CompilerParams(vmem_limit_bytes=VMEM_LIMIT),
        cost_estimate=cost,
        name=name,
    )


def array(*shape):
    return jax.ShapeDtypeStruct(shape, jnp.float32)


def after(rows):
    return pltpu.roll(rows, rows.shape[0] - 1, 0)


def before(rows):
    return pltpu.roll(rows, 1, 0)


def lift_rows(line, target, at, forward, place):
    cells = 128
    pairs = cells // 2
    wide = pairs + 8
    s = line[pl.ds(MARGIN + at - 8, wide, stride=2), :]
    d = line[pl.ds(MARGIN + at - 7, wide, stride=2), :]
    if forward:
        d = d + A * (s + after(s))
        s = s + B * (before(d) + d)
        d = d + C * (s + after(s))
        s = s + E * (before(d) + d)
        s = s * (1.0 / BALANCE)
        d = d * BALANCE
    else:
        s = s * BALANCE
        d = d * (1.0 / BALANCE)
        s = s - E * (before(d) + d)
        d = d - C * (s + after(s))
        s = s - B * (before(d) + d)
        d = d - A * (s + after(s))
    block = target.shape[0] // len(place)
    half = block // 2
    for k in range(cells // block):
        to = place[at // block + k] * block
        target[pl.ds(to, half, stride=2), :] = s[4 + k * half : 4 + (k + 1) * half]
        target[pl.ds(to + 1, half, stride=2), :] = d[4 + k * half : 4 + (k + 1) * half]


def mirror_start(line):
    for k in range(1, 9):
        line[pl.ds(MARGIN - k, 1), :] = line[pl.ds(MARGIN + k, 1), :]


def mirror_end(line, ny):
    for k in range(1, 9):
        line[pl.ds(MARGIN + ny - 1 + k, 1), :] = line[pl.ds(MARGIN + ny - 1 - k, 1), :]


def analyse_kernel(order, source, target, line, arrived):
    ny = source.shape[0]
    n = ny // CHUNK
    copies = []
    for k in range(n):
        inner = pl.ds(MARGIN + k * CHUNK, CHUNK)
        rows = pl.ds(k * CHUNK, CHUNK)
        copies.append(pltpu.make_async_copy(source.at[rows], line.at[inner], arrived.at[k]))
        copies[k].start()
    copies[0].wait()
    mirror_start(line)
    for k in range(n):
        if k + 1 < n:
            copies[k + 1].wait()
        else:
            mirror_end(line, ny)
        for at in range(k * CHUNK, (k + 1) * CHUNK, 128):
            lift_rows(line, target, at, True, places(order))


def analyse_columns(order, values):
    ny = values.shape[0]
    values = pltpu.with_memory_space_constraint(values, pltpu.HBM)
    scratch = [
        pltpu.VMEM((ny + 2 * MARGIN, X), jnp.float32),
        pltpu.SemaphoreType.DMA((ny // CHUNK,)),
    ]
    out_shape = pltpu.VMEM((ny, X), jnp.float32)
    kernel = functools.partial(analyse_kernel, order)
    return call(kernel, out_shape, [pltpu.HBM], scratch, "analyse_y")(values)


def synthesise_kernel(order, source, target, line, lifted, left):
    ny = source.shape[0]
    n = ny // CHUNK
    block = ny // len(order)
    for k, device in enumerate(order):
        line[pl.ds(MARGIN + device * block, block), :] = source[pl.ds(k * block, block), :]
    mirror_start(line)
    mirror_end(line, ny)
    copies = []
    for k in range(n):
        for at in range(k * CHUNK, (k + 1) * CHUNK, 128):
            lift_rows(line, lifted, at, False, range(len(order)))
        rows = pl.ds(k * CHUNK, CHUNK)
        copies.append(pltpu.make_async_copy(lifted.at[rows], target.at[rows], left.at[k]))
        copies[k].start()
    for copy in copies:
        copy.wait()


def synthesise_columns(order, values):
    ny = values.shape[0]
    scratch = [
        pltpu.VMEM((ny + 2 * MARGIN, X), jnp.float32),
        pltpu.VMEM((ny, X), jnp.float32),
        pltpu.SemaphoreType.DMA((ny // CHUNK,)),
    ]
    kernel = functools.partial(synthesise_kernel, order)
    return call(kernel, array(ny, X), [pltpu.VMEM], scratch, "synthesise_y", pltpu.HBM)(values)


def edge_kernel(values, to_left, to_right, edges):
    cells = values.shape[0]
    for at in range(0, cells, X):
        turned = values[pl.ds(at, X), :].T
        edges[0:EDGE, pl.ds(at, X)] = turned[:EDGE]
        edges[EDGE : 2 * EDGE, pl.ds(at, X)] = turned[X - EDGE :]

    def cell(k):
        return edges[pl.ds(k, 1), :]

    s = [cell(2 * n) for n in range(EDGE)]
    d = [cell(2 * n + 1) for n in range(EDGE)]
    d1 = {n: d[n] + A * (s[n] + s[n + 1]) for n in (0, 1, 2, 5, 6)}
    s1 = {n: s[n] + B * (d1[n - 1] + d1[n]) for n in (1, 2, 6)}
    to_left[0:1] = s[0]
    to_left[1:2] = d1[0]
    to_left[2:3] = s1[1]
    to_left[3:4] = d1[1] + C * (s1[1] + s1[2])
    to_right[0:1] = d[7] + A * s[7]
    to_right[1:2] = s[7] + B * d1[6]
    to_right[2:3] = d1[6] + C * s1[6]
    to_right[3:4] = jnp.zeros_like(s[0])


def edges_of(values):
    cells = values.shape[0]
    shapes = (array(4, cells), array(4, cells), array(2 * EDGE, cells))
    return call(edge_kernel, shapes, [pltpu.VMEM], name="edges_x")(values)


def analyse_depth(cells):
    n = len(cells) // 2
    s, d = cells[0::2], cells[1::2]

    def right(k):
        return s[min(k + 1, n - 1)]

    def left(k):
        return d[max(k - 1, 0)]

    d = [d[k] + A * (s[k] + right(k)) for k in range(n)]
    s = [s[k] + B * (left(k) + d[k]) for k in range(n)]
    d = [d[k] + C * (s[k] + right(k)) for k in range(n)]
    s = [s[k] + E * (left(k) + d[k]) for k in range(n)]
    return s, d


def synthesise_depth(s, d):
    n = len(s)

    def right(k):
        return s[min(k + 1, n - 1)]

    def left(k):
        return d[max(k - 1, 0)]

    s = [s[k] - E * (left(k) + d[k]) for k in range(n)]
    d = [d[k] - C * (s[k] + right(k)) for k in range(n)]
    s = [s[k] - B * (left(k) + d[k]) for k in range(n)]
    d = [d[k] - A * (s[k] + right(k)) for k in range(n)]
    return [v for pair in zip(s, d) for v in pair]


def gain_tables(gains, y_odd, x_odd):
    tables = []
    for z in range(2):
        low = jnp.where(x_odd, gains[z, 0, 1], gains[z, 0, 0])
        high = jnp.where(x_odd, gains[z, 1, 1], gains[z, 1, 0])
        tables.append(jnp.where(y_odd, high, low))
    return tables


def scale_tables(x_odd):
    along = jnp.where(x_odd, BALANCE, 1.0 / BALANCE)
    return along * (1.0 / BALANCE), along * BALANCE


def dot(left, right):
    return jnp.dot(left, right, precision=lax.Precision.HIGHEST, preferred_element_type=jnp.float32)


def split(values):
    first = values.astype(jnp.bfloat16)
    rest = values - first.astype(jnp.float32)
    second = rest.astype(jnp.bfloat16)
    third = (rest - second.astype(jnp.float32)).astype(jnp.bfloat16)
    return first, second, third


def split_matrix(matrix):
    matrix = np.asarray(matrix, np.float32)
    first = matrix.astype(jnp.bfloat16)
    rest = matrix - first.astype(np.float32)
    second = rest.astype(jnp.bfloat16)
    third = (rest - second.astype(np.float32)).astype(jnp.bfloat16)
    wide = np.concatenate([np.concatenate([first, second], 1)] * 2, 0)
    return jnp.asarray(wide), jnp.asarray(np.concatenate([third, first], 0))


def split_dot(values, wide, tall):
    first, second, third = split(values)
    large = jnp.dot(jnp.concatenate([first, second], 1), wide, preferred_element_type=jnp.float32)
    small = jnp.dot(jnp.concatenate([first, third], 1), tall, preferred_element_type=jnp.float32)
    return large[:, :X] + (large[:, X:] + small)


def end_kind(blocks):
    index = lax.axis_index("ba")
    return 2 * (index == 0).astype(jnp.int32) + (index == blocks - 1).astype(jnp.int32)


def main_kernel(
    blocks, order, values, gains, edges, forward, forward_tall, backward, backward_tall, weights,
    coefficients, rebuilt, own_rows,
):
    own_rows[...] = dot(weights[end_kind(blocks)], edges[...])
    nz, ny, _ = values.shape
    place = places(order)
    lane = lax.broadcasted_iota(jnp.int32, (ROWS, X), 1)
    row = lax.broadcasted_iota(jnp.int32, (ROWS, X), 0)
    gain_low, gain_high = gain_tables(gains, row % 2 == 1, lane % 2 == 1)
    scale_low, scale_high = scale_tables(lane % 2 == 1)
    lines = split_dot(values[...].reshape(nz * ny, X), forward[...], forward_tall[...])
    rebuilt[...] = lines.reshape(nz, ny, X)

    def body(k, carry):
        rows = pl.ds(pl.multiple_of(k * ROWS, ROWS), ROWS)
        s, d = analyse_depth([rebuilt[place[z], rows, :] for z in range(nz)])
        for n in range(nz // 2):
            coefficients[2 * n, rows, :] = s[n] * scale_low
            coefficients[2 * n + 1, rows, :] = d[n] * scale_high
        cells = synthesise_depth([v * gain_low for v in s], [v * gain_high for v in d])
        for z in range(nz):
            rebuilt[place[z], rows, :] = cells[z]
        return carry

    lax.fori_loop(0, ny // ROWS, body, 0)
    lines = split_dot(rebuilt[...].reshape(nz * ny, X), backward[...], backward_tall[...])
    rebuilt[...] = lines.reshape(nz, ny, X)


def correction_kinds():
    return np.stack([correction_matrix(a, b) for a in (False, True) for b in (False, True)])


def main_depths(blocks, order, values, gains, edges):
    shape = array(*values.shape)
    size = values.size
    cost = pl.CostEstimate(flops=100 * size, bytes_accessed=12 * size, transcendentals=0)
    spaces = [pltpu.VMEM, pltpu.SMEM] + [pltpu.VMEM] * 6
    weights = jnp.asarray(correction_kinds()[:, :, 8:], jnp.float32)
    forward = split_matrix(own_analysis_matrix())
    backward = split_matrix(synthesis_matrix()[:, :X].T)
    kernel = functools.partial(main_kernel, blocks, order)
    shapes = (shape, shape, array(*edges.shape))
    return call(kernel, shapes, spaces, name="depth_main", cost=cost)(
        values, gains, edges, *forward, *backward, weights
    )


def halo_kernel(
    blocks, order, own_coefficients, own_rebuilt, from_right, from_left, own_rows, gains, weights, spread,
    coefficients, rebuilt, held, left,
):
    nz = own_rebuilt.shape[0]
    kind = end_kind(blocks)
    weight = [weights[kind, :, k * X : (k + 1) * X] for k in range(7)]

    def rows_of(at):
        found = own_rows[:, at : at + X]
        for k in range(7):
            source, row = (from_right, k) if k < 4 else (from_left, k - 4)
            halo = source[row : row + 1, at : at + X]
            found = found + weight[k] * jnp.broadcast_to(halo, (16, X))
        return found

    lane = lax.broadcasted_iota(jnp.int32, (ROWS, X), 1)
    row = lax.broadcasted_iota(jnp.int32, (ROWS, X), 0)
    low = lane < HALF
    low_16 = lax.broadcasted_iota(jnp.int32, (16, X), 1) < HALF
    cells = []
    for k in range(nz // 2):
        found = rows_of(k * X)
        inside, beyond = found[0:8], found[8:16]
        cells.append(jnp.where(low, inside, pltpu.roll(beyond, HALF, 1)))
        cells.append(jnp.where(low, pltpu.roll(inside, HALF, 1), beyond))
    x_odd = (row + jnp.where(low | (row < 4), 0, 1)) % 2 == 1
    gain_low, gain_high = gain_tables(gains, lane % 2 == 1, x_odd)
    scale_low, scale_high = scale_tables(x_odd)
    s, d = analyse_depth([cells[k] for k in places(order)])
    middle = jnp.zeros((X - 16, X), jnp.float32)
    copies = []
    for k in range(nz // 2):
        both = jnp.where(low, s[k] * scale_low, pltpu.roll(d[k] * scale_high, HALF, 1))
        ends = [jnp.where(row < 4, both, 0.0), middle, jnp.where(row < 4, 0.0, both)]
        turned = jnp.concatenate(ends, 0).T
        held[2 * k] = own_coefficients[2 * k] + turned[:HALF]
        held[2 * k + 1] = own_coefficients[2 * k + 1] + turned[HALF:]
        if k % 2 == 1:
            part = pl.ds(2 * k - 2, 4)
            copies.append(pltpu.make_async_copy(held.at[part], coefficients.at[part], left.at[k // 2]))
            copies[-1].start()
    cells = synthesise_depth([v * gain_low for v in s], [v * gain_high for v in d])
    table = [spread[:, k * X : (k + 1) * X] for k in range(8)]
    for k in range(nz // 2):
        mixed = []
        for v in (cells[order[2 * k]], cells[order[2 * k + 1]]):
            total = None
            for m in range(8):
                term = table[m] * jnp.broadcast_to(v[m : m + 1], (16, X))
                total = term if total is None else total + term
            mixed.append(total + pltpu.roll(total, HALF, 1))
        both = jnp.where(low_16, *mixed)
        turned = jnp.concatenate([both[:8], middle, both[8:]], 0).T
        rebuilt[2 * k] = own_rebuilt[2 * k] + turned[:HALF]
        rebuilt[2 * k + 1] = own_rebuilt[2 * k + 1] + turned[HALF:]
    for copy in copies:
        copy.wait()


def add_halo(blocks, order, own_coefficients, own_rebuilt, from_right, from_left, own_rows, gains):
    shape = own_rebuilt.shape
    nz = shape[0]
    weights = np.repeat(correction_kinds()[:, :, :7], X, 2)
    mixing = edge_synthesis_matrix()
    spread = np.zeros((16, 8, X))
    spread[:, :, :HALF] = mixing[:, :8, None]
    spread[:, :, HALF:] = mixing[:, 8:, None]
    spaces = [pltpu.VMEM] * 5 + [pltpu.SMEM] + [pltpu.VMEM] * 2
    scratch = [pltpu.VMEM(shape, jnp.float32), pltpu.SemaphoreType.DMA((nz // 4,))]
    kernel = functools.partial(halo_kernel, blocks, order)
    out_space = (pltpu.HBM, pltpu.VMEM)
    return call(kernel, (array(*shape), array(*shape)), spaces, scratch, "depth_halo", out_space)(
        own_coefficients, own_rebuilt, from_right, from_left, own_rows, gains,
        jnp.asarray(weights, jnp.float32), jnp.asarray(spread.reshape(16, 8 * X), jnp.float32),
    )


def per_device(blocks, field, gains):
    nz = lax.axis_size("aa")
    ny = field.shape[1]
    order = exchange_order(nz)

    def exchange(blocks_):
        blocks_ = blocks_.reshape(nz, ny // nz, X)
        return lax.all_to_all(blocks_, "aa", 0, 0, axis_index_groups=[order], tiled=True)

    by_depth = exchange(analyse_columns(order, field.reshape(ny, X)))
    to_left, to_right, edges = edges_of(by_depth.reshape(ny, X))
    from_right = lax.ppermute(to_left, "ba", [(k, k - 1) for k in range(1, blocks)])
    from_left = lax.ppermute(to_right, "ba", [(k, k + 1) for k in range(blocks - 1)])
    own_coefficients, own_rebuilt, own_rows = main_depths(blocks, order, by_depth, gains, edges)
    coefficients, rebuilt = add_halo(
        blocks, order, own_coefficients, own_rebuilt, from_right, from_left, own_rows, gains
    )
    rebuilt = synthesise_columns(order, exchange(rebuilt).reshape(ny, X))
    return coefficients, rebuilt.reshape(1, ny, X)


def solution(mesh):
    return jax.shard_map(
        functools.partial(per_device, mesh.shape["ba"]),
        mesh=mesh,
        in_specs=(P("aa", None, "ba"), P()),
        out_specs=(P(None, "aa", "ba"), P("aa", None, "ba")),
        check_vma=False,
    )
```

```python
import functools

import jax
import jax.numpy as jnp
import numpy as np
from jax import lax
from jax.experimental import pallas as pl
from jax.experimental.pallas import tpu as pltpu
from jax.sharding import PartitionSpec as P

PREDICT_FIRST = -1.586134342059924
UPDATE_FIRST = -0.052980118572961
PREDICT_SECOND = 0.882911075530934
UPDATE_SECOND = 0.443506852043971
BALANCE = 1.230174104914001
A, B, C, E = PREDICT_FIRST, UPDATE_FIRST, PREDICT_SECOND, UPDATE_SECOND

X = 128
HALF = X // 2
ROWS = 8
MARGIN = 16
CHUNK = 256
VMEM_LIMIT = 24 * 1024 * 1024
EDGE = 8
HIGHEST = lax.Precision.HIGHEST

def exchange_order(n):
    if n != 32:
        return [(k + 2) % n for k in range(n)]

    def where(k):
        return k // 8, k // 2 % 4, k % 2

    first = 11

    def distance(k):
        (x, y, core), (x_first, y_first, core_first) = where(k), where(first)
        along = abs(x - x_first)
        return 10 * (min(along, 4 - along) + abs(y - y_first)) + (core != core_first)

    rest = [k for k in range(n) if k != first]
    rest = sorted(rest, key=lambda k: -distance(k))
    return [first, *rest[22:], *rest[:22]]


def places(order):
    out = [0] * len(order)
    for k, device in enumerate(order):
        out[device] = k
    return out


def edge_matrix():
    unit = np.eye(X)
    s, d = unit[0::2], unit[1::2]
    d1 = [d[n] + A * (s[n] + s[n + 1]) for n in range(HALF - 1)]
    s1 = [None] + [s[n] + B * (d1[n - 1] + d1[n]) for n in range(1, HALF - 1)]
    last = HALF - 1
    out = np.zeros((16, X))
    out[0] = s[0]
    out[1] = d1[0]
    out[2] = s1[1]
    out[3] = d1[1] + C * (s1[1] + s1[2])
    out[4] = d[last] + A * s[last]
    out[5] = s[last] + B * d1[last - 1]
    out[6] = d1[last - 1] + C * s1[last - 1]
    out[8] = d[0] + A * s[1]
    out[9] = s[1] + B * d1[1]
    out[10] = d1[1] + C * s1[2]
    out[12] = s[last]
    out[13] = d1[last - 1]
    out[14] = s1[last - 1]
    out[15] = d1[last - 2] + C * (s1[last - 2] + s1[last - 1])
    return np.concatenate([out[:, :EDGE], out[:, X - EDGE :]], 1)


def correction_matrix(left_end, right_end):
    unit = np.eye(24)
    own = unit[8:]
    h0, h1, h2, h3 = own[12:16] if right_end else unit[0:4]
    hp, hq, hr = own[8:11] if left_end else unit[4:7]
    s0, d10, p, q = own[0], own[1], own[4], own[5]
    add_d1 = A * h0
    d1 = p + add_d1
    s1_next = h0 + B * (d1 + h1)
    add_s1 = B * add_d1
    add_d2 = add_d1 + C * (add_s1 + s1_next)
    add_d2_before = C * add_s1
    add_s2 = add_s1 + E * (add_d2_before + add_d2)
    add_s2_before = E * add_d2_before
    s1 = q + B * d1
    d2 = d1 + C * (s1 + s1_next)
    d2_next = h1 + C * (s1_next + h2)
    s2_next = s1_next + E * (d2 + d2_next)
    s2_after = h2 + E * (d2_next + h3)
    right = [add_s2_before, add_d2_before, add_s2, add_d2]
    right_beyond = [s2_next, d2_next, s2_after, h3]
    d1_out = hp + A * s0
    s1_out = hq + B * d1_out
    add_s1 = B * d1_out
    s1 = s0 + B * (d1_out + d10)
    add_d2 = C * add_s1
    d2_out = d1_out + C * (s1_out + s1)
    d2_far = hr + C * s1_out
    s2_out = s1_out + E * (d2_far + d2_out)
    left = [add_s1 + E * (d2_out + add_d2), add_d2, E * add_d2, 0 * s0]
    left_beyond = [d2_out, s2_out, d2_far, 0 * s0]
    found = np.stack(left + right + right_beyond + left_beyond)
    return np.concatenate([found[:, :8], found[:, 8:] @ edge_matrix()], 1)


def own_analysis_matrix():
    unit = np.eye(X)
    zero = np.zeros((1, X))
    s, d = unit[0::2], unit[1::2]
    d = d + A * (s + np.concatenate([s[1:], zero]))
    s = s + B * (d + np.concatenate([zero, d[:-1]]))
    d = d + C * (s + np.concatenate([s[1:], zero]))
    s = s + E * (d + np.concatenate([zero, d[:-1]]))
    out = np.zeros((X, X))
    out[:, 0::2] = s.T
    out[:, 1::2] = d.T
    return out


def synthesis_matrix():
    unit = np.eye(X + 8)
    place = {k: k for k in range(X + 4)}
    place.update({-1: X + 4, -2: X + 5, -3: X + 6})
    n_all = HALF
    s2 = {n: unit[place[2 * n]] for n in range(-1, n_all + 2)}
    d2 = {n: unit[place[2 * n + 1]] for n in range(-2, n_all + 2)}
    s1 = {n: s2[n] - E * (d2[n - 1] + d2[n]) for n in range(-1, n_all + 2)}
    d1 = {n: d2[n] - C * (s1[n] + s1[n + 1]) for n in range(-1, n_all + 1)}
    s = {n: s1[n] - B * (d1[n - 1] + d1[n]) for n in range(n_all + 1)}
    d = {n: d1[n] - A * (s[n] + s[n + 1]) for n in range(n_all)}
    cells = np.zeros((X, X + 8))
    cells[0::2] = [s[n] for n in range(n_all)]
    cells[1::2] = [d[n] for n in range(n_all)]
    return cells


def edge_synthesis_matrix():
    inside = [0, 1, 2, 3, 124, 125, 126, 127] + [X + k for k in range(8)]
    return synthesis_matrix()[list(range(8)) + list(range(120, 128))][:, inside]


def call(kernel, out_shape, spaces, scratch=(), name=None, out_space=pltpu.VMEM, cost=None):
    if isinstance(out_space, tuple):
        out_specs = tuple(pl.BlockSpec(memory_space=space) for space in out_space)
    else:
        out_specs = jax.tree.map(lambda _: pl.BlockSpec(memory_space=out_space), out_shape)
    return pl.pallas_call(
        kernel,
        out_shape=out_shape,
        in_specs=[pl.BlockSpec(memory_space=space) for space in spaces],
        out_specs=out_specs,
        scratch_shapes=list(scratch),
        compiler_params=pltpu.CompilerParams(vmem_limit_bytes=VMEM_LIMIT),
        cost_estimate=cost,
        name=name,
    )


def array(*shape):
    return jax.ShapeDtypeStruct(shape, jnp.float32)


def after(rows):
    return pltpu.roll(rows, rows.shape[0] - 1, 0)


def before(rows):
    return pltpu.roll(rows, 1, 0)


def lift_rows(line, target, at, forward, place):
    cells = 128
    pairs = cells // 2
    wide = pairs + 8
    s = line[pl.ds(MARGIN + at - 8, wide, stride=2), :]
    d = line[pl.ds(MARGIN + at - 7, wide, stride=2), :]
    if forward:
        d = d + A * (s + after(s))
        s = s + B * (before(d) + d)
        d = d + C * (s + after(s))
        s = s + E * (before(d) + d)
        s = s * (1.0 / BALANCE)
        d = d * BALANCE
    else:
        s = s * BALANCE
        d = d * (1.0 / BALANCE)
        s = s - E * (before(d) + d)
        d = d - C * (s + after(s))
        s = s - B * (before(d) + d)
        d = d - A * (s + after(s))
    block = target.shape[0] // len(place)
    half = block // 2
    for k in range(cells // block):
        to = place[at // block + k] * block
        target[pl.ds(to, half, stride=2), :] = s[4 + k * half : 4 + (k + 1) * half]
        target[pl.ds(to + 1, half, stride=2), :] = d[4 + k * half : 4 + (k + 1) * half]


def mirror_start(line):
    for k in range(1, 9):
        line[pl.ds(MARGIN - k, 1), :] = line[pl.ds(MARGIN + k, 1), :]


def mirror_end(line, ny):
    for k in range(1, 9):
        line[pl.ds(MARGIN + ny - 1 + k, 1), :] = line[pl.ds(MARGIN + ny - 1 - k, 1), :]


def analyse_kernel(order, source, target, line, arrived):
    ny = source.shape[0]
    n = ny // CHUNK
    copies = []
    for k in range(n):
        inner = pl.ds(MARGIN + k * CHUNK, CHUNK)
        rows = pl.ds(k * CHUNK, CHUNK)
        copies.append(pltpu.make_async_copy(source.at[rows], line.at[inner], arrived.at[k]))
        copies[k].start()
    copies[0].wait()
    mirror_start(line)
    for k in range(n):
        if k + 1 < n:
            copies[k + 1].wait()
        else:
            mirror_end(line, ny)
        for at in range(k * CHUNK, (k + 1) * CHUNK, 128):
            lift_rows(line, target, at, True, places(order))


def analyse_columns(order, values):
    ny = values.shape[0]
    values = pltpu.with_memory_space_constraint(values, pltpu.HBM)
    scratch = [
        pltpu.VMEM((ny + 2 * MARGIN, X), jnp.float32),
        pltpu.SemaphoreType.DMA((ny // CHUNK,)),
    ]
    out_shape = pltpu.VMEM((ny, X), jnp.float32)
    kernel = functools.partial(analyse_kernel, order)
    return call(kernel, out_shape, [pltpu.HBM], scratch, "analyse_y")(values)


def synthesise_kernel(order, source, target, line, lifted, left):
    ny = source.shape[0]
    n = ny // CHUNK
    block = ny // len(order)
    for k, device in enumerate(order):
        line[pl.ds(MARGIN + device * block, block), :] = source[pl.ds(k * block, block), :]
    mirror_start(line)
    mirror_end(line, ny)
    copies = []
    for k in range(n):
        for at in range(k * CHUNK, (k + 1) * CHUNK, 128):
            lift_rows(line, lifted, at, False, range(len(order)))
        rows = pl.ds(k * CHUNK, CHUNK)
        copies.append(pltpu.make_async_copy(lifted.at[rows], target.at[rows], left.at[k]))
        copies[k].start()
    for copy in copies:
        copy.wait()


def synthesise_columns(order, values):
    ny = values.shape[0]
    scratch = [
        pltpu.VMEM((ny + 2 * MARGIN, X), jnp.float32),
        pltpu.VMEM((ny, X), jnp.float32),
        pltpu.SemaphoreType.DMA((ny // CHUNK,)),
    ]
    kernel = functools.partial(synthesise_kernel, order)
    return call(kernel, array(ny, X), [pltpu.VMEM], scratch, "synthesise_y", pltpu.HBM)(values)


def edge_kernel(values, to_left, to_right, edges):
    cells = values.shape[0]
    for at in range(0, cells, X):
        turned = values[pl.ds(at, X), :].T
        edges[0:EDGE, pl.ds(at, X)] = turned[:EDGE]
        edges[EDGE : 2 * EDGE, pl.ds(at, X)] = turned[X - EDGE :]

    def cell(k):
        return edges[pl.ds(k, 1), :]

    s = [cell(2 * n) for n in range(EDGE)]
    d = [cell(2 * n + 1) for n in range(EDGE)]
    d1 = {n: d[n] + A * (s[n] + s[n + 1]) for n in (0, 1, 2, 5, 6)}
    s1 = {n: s[n] + B * (d1[n - 1] + d1[n]) for n in (1, 2, 6)}
    to_left[0:1] = s[0]
    to_left[1:2] = d1[0]
    to_left[2:3] = s1[1]
    to_left[3:4] = d1[1] + C * (s1[1] + s1[2])
    to_right[0:1] = d[7] + A * s[7]
    to_right[1:2] = s[7] + B * d1[6]
    to_right[2:3] = d1[6] + C * s1[6]
    to_right[3:4] = jnp.zeros_like(s[0])


def edges_of(values):
    cells = values.shape[0]
    shapes = (array(4, cells), array(4, cells), array(2 * EDGE, cells))
    return call(edge_kernel, shapes, [pltpu.VMEM], name="edges_x")(values)


def analyse_depth(cells):
    n = len(cells) // 2
    s, d = cells[0::2], cells[1::2]

    def right(k):
        return s[min(k + 1, n - 1)]

    def left(k):
        return d[max(k - 1, 0)]

    d = [d[k] + A * (s[k] + right(k)) for k in range(n)]
    s = [s[k] + B * (left(k) + d[k]) for k in range(n)]
    d = [d[k] + C * (s[k] + right(k)) for k in range(n)]
    s = [s[k] + E * (left(k) + d[k]) for k in range(n)]
    return s, d


def synthesise_depth(s, d):
    n = len(s)

    def right(k):
        return s[min(k + 1, n - 1)]

    def left(k):
        return d[max(k - 1, 0)]

    s = [s[k] - E * (left(k) + d[k]) for k in range(n)]
    d = [d[k] - C * (s[k] + right(k)) for k in range(n)]
    s = [s[k] - B * (left(k) + d[k]) for k in range(n)]
    d = [d[k] - A * (s[k] + right(k)) for k in range(n)]
    return [v for pair in zip(s, d) for v in pair]


def gain_tables(gains, y_odd, x_odd):
    tables = []
    for z in range(2):
        low = jnp.where(x_odd, gains[z, 0, 1], gains[z, 0, 0])
        high = jnp.where(x_odd, gains[z, 1, 1], gains[z, 1, 0])
        tables.append(jnp.where(y_odd, high, low))
    return tables


def scale_tables(x_odd):
    along = jnp.where(x_odd, BALANCE, 1.0 / BALANCE)
    return along * (1.0 / BALANCE), along * BALANCE


def dot(left, right):
    return jnp.dot(left, right, precision=lax.Precision.HIGHEST, preferred_element_type=jnp.float32)


def split(values):
    first = values.astype(jnp.bfloat16)
    rest = values - first.astype(jnp.float32)
    second = rest.astype(jnp.bfloat16)
    third = (rest - second.astype(jnp.float32)).astype(jnp.bfloat16)
    return first, second, third


def split_matrix(matrix):
    matrix = np.asarray(matrix, np.float32)
    first = matrix.astype(jnp.bfloat16)
    rest = matrix - first.astype(np.float32)
    second = rest.astype(jnp.bfloat16)
    third = (rest - second.astype(np.float32)).astype(jnp.bfloat16)
    wide = np.concatenate([np.concatenate([first, second], 1)] * 2, 0)
    return jnp.asarray(wide), jnp.asarray(np.concatenate([third, first], 0))


def split_dot(values, wide, tall):
    first, second, third = split(values)
    large = jnp.dot(jnp.concatenate([first, second], 1), wide, preferred_element_type=jnp.float32)
    small = jnp.dot(jnp.concatenate([first, third], 1), tall, preferred_element_type=jnp.float32)
    return large[:, :X] + (large[:, X:] + small)


def end_kind(blocks):
    index = lax.axis_index("ba")
    return 2 * (index == 0).astype(jnp.int32) + (index == blocks - 1).astype(jnp.int32)


def main_kernel(
    blocks, order, values, gains, edges, forward, forward_tall, backward, backward_tall, weights,
    coefficients, rebuilt, own_rows,
):
    own_rows[...] = dot(weights[end_kind(blocks)], edges[...])
    nz, ny, _ = values.shape
    place = places(order)
    lane = lax.broadcasted_iota(jnp.int32, (ROWS, X), 1)
    row = lax.broadcasted_iota(jnp.int32, (ROWS, X), 0)
    gain_low, gain_high = gain_tables(gains, row % 2 == 1, lane % 2 == 1)
    scale_low, scale_high = scale_tables(lane % 2 == 1)
    lines = split_dot(values[...].reshape(nz * ny, X), forward[...], forward_tall[...])
    rebuilt[...] = lines.reshape(nz, ny, X)

    def body(k, carry):
        rows = pl.ds(pl.multiple_of(k * ROWS, ROWS), ROWS)
        s, d = analyse_depth([rebuilt[place[z], rows, :] for z in range(nz)])
        for n in range(nz // 2):
            coefficients[2 * n, rows, :] = s[n] * scale_low
            coefficients[2 * n + 1, rows, :] = d[n] * scale_high
        cells = synthesise_depth([v * gain_low for v in s], [v * gain_high for v in d])
        for z in range(nz):
            rebuilt[place[z], rows, :] = cells[z]
        return carry

    lax.fori_loop(0, ny // ROWS, body, 0)
    lines = split_dot(rebuilt[...].reshape(nz * ny, X), backward[...], backward_tall[...])
    rebuilt[...] = lines.reshape(nz, ny, X)


def correction_kinds():
    return np.stack([correction_matrix(a, b) for a in (False, True) for b in (False, True)])


def main_depths(blocks, order, values, gains, edges):
    shape = array(*values.shape)
    size = values.size
    cost = pl.CostEstimate(flops=100 * size, bytes_accessed=12 * size, transcendentals=0)
    spaces = [pltpu.VMEM, pltpu.SMEM] + [pltpu.VMEM] * 6
    weights = jnp.asarray(correction_kinds()[:, :, 8:], jnp.float32)
    forward = split_matrix(own_analysis_matrix())
    backward = split_matrix(synthesis_matrix()[:, :X].T)
    kernel = functools.partial(main_kernel, blocks, order)
    shapes = (shape, shape, array(*edges.shape))
    return call(kernel, shapes, spaces, name="depth_main", cost=cost)(
        values, gains, edges, *forward, *backward, weights
    )


def halo_kernel(
    blocks, order, own_coefficients, own_rebuilt, from_right, from_left, own_rows, gains, weights, spread,
    coefficients, rebuilt, held, left,
):
    nz = own_rebuilt.shape[0]
    kind = end_kind(blocks)
    weight = [weights[kind, :, k * X : (k + 1) * X] for k in range(7)]

    def rows_of(at):
        found = own_rows[:, at : at + X]
        for k in range(7):
            source, row = (from_right, k) if k < 4 else (from_left, k - 4)
            halo = source[row : row + 1, at : at + X]
            found = found + weight[k] * jnp.broadcast_to(halo, (16, X))
        return found

    lane = lax.broadcasted_iota(jnp.int32, (ROWS, X), 1)
    row = lax.broadcasted_iota(jnp.int32, (ROWS, X), 0)
    low = lane < HALF
    low_16 = lax.broadcasted_iota(jnp.int32, (16, X), 1) < HALF
    cells = []
    for k in range(nz // 2):
        found = rows_of(k * X)
        inside, beyond = found[0:8], found[8:16]
        cells.append(jnp.where(low, inside, pltpu.roll(beyond, HALF, 1)))
        cells.append(jnp.where(low, pltpu.roll(inside, HALF, 1), beyond))
    x_odd = (row + jnp.where(low | (row < 4), 0, 1)) % 2 == 1
    gain_low, gain_high = gain_tables(gains, lane % 2 == 1, x_odd)
    scale_low, scale_high = scale_tables(x_odd)
    s, d = analyse_depth([cells[k] for k in places(order)])
    middle = jnp.zeros((X - 16, X), jnp.float32)
    copies = []
    for k in range(nz // 2):
        both = jnp.where(low, s[k] * scale_low, pltpu.roll(d[k] * scale_high, HALF, 1))
        ends = [jnp.where(row < 4, both, 0.0), middle, jnp.where(row < 4, 0.0, both)]
        turned = jnp.concatenate(ends, 0).T
        held[2 * k] = own_coefficients[2 * k] + turned[:HALF]
        held[2 * k + 1] = own_coefficients[2 * k + 1] + turned[HALF:]
        if k % 2 == 1:
            part = pl.ds(2 * k - 2, 4)
            copies.append(pltpu.make_async_copy(held.at[part], coefficients.at[part], left.at[k // 2]))
            copies[-1].start()
    cells = synthesise_depth([v * gain_low for v in s], [v * gain_high for v in d])
    table = [spread[:, k * X : (k + 1) * X] for k in range(8)]
    for k in range(nz // 2):
        mixed = []
        for v in (cells[order[2 * k]], cells[order[2 * k + 1]]):
            total = None
            for m in range(8):
                term = table[m] * jnp.broadcast_to(v[m : m + 1], (16, X))
                total = term if total is None else total + term
            mixed.append(total + pltpu.roll(total, HALF, 1))
        both = jnp.where(low_16, *mixed)
        turned = jnp.concatenate([both[:8], middle, both[8:]], 0).T
        rebuilt[2 * k] = own_rebuilt[2 * k] + turned[:HALF]
        rebuilt[2 * k + 1] = own_rebuilt[2 * k + 1] + turned[HALF:]
    for copy in copies:
        copy.wait()


def add_halo(blocks, order, own_coefficients, own_rebuilt, from_right, from_left, own_rows, gains):
    shape = own_rebuilt.shape
    nz = shape[0]
    weights = np.repeat(correction_kinds()[:, :, :7], X, 2)
    mixing = edge_synthesis_matrix()
    spread = np.zeros((16, 8, X))
    spread[:, :, :HALF] = mixing[:, :8, None]
    spread[:, :, HALF:] = mixing[:, 8:, None]
    spaces = [pltpu.VMEM] * 5 + [pltpu.SMEM] + [pltpu.VMEM] * 2
    scratch = [pltpu.VMEM(shape, jnp.float32), pltpu.SemaphoreType.DMA((nz // 4,))]
    kernel = functools.partial(halo_kernel, blocks, order)
    out_space = (pltpu.HBM, pltpu.VMEM)
    return call(kernel, (array(*shape), array(*shape)), spaces, scratch, "depth_halo", out_space)(
        own_coefficients, own_rebuilt, from_right, from_left, own_rows, gains,
        jnp.asarray(weights, jnp.float32), jnp.asarray(spread.reshape(16, 8 * X), jnp.float32),
    )


def per_device(blocks, field, gains):
    nz = lax.axis_size("aa")
    ny = field.shape[1]
    order = exchange_order(nz)

    def exchange(blocks_):
        blocks_ = blocks_.reshape(nz, ny // nz, X)
        return lax.all_to_all(blocks_, "aa", 0, 0, axis_index_groups=[order], tiled=True)

    by_depth = exchange(analyse_columns(order, field.reshape(ny, X)))
    to_left, to_right, edges = edges_of(by_depth.reshape(ny, X))
    from_right = lax.ppermute(to_left, "ba", [(k, k - 1) for k in range(1, blocks)])
    from_left = lax.ppermute(to_right, "ba", [(k, k + 1) for k in range(blocks - 1)])
    own_coefficients, own_rebuilt, own_rows = main_depths(blocks, order, by_depth, gains, edges)
    coefficients, rebuilt = add_halo(
        blocks, order, own_coefficients, own_rebuilt, from_right, from_left, own_rows, gains
    )
    rebuilt = synthesise_columns(order, exchange(rebuilt).reshape(ny, X))
    return coefficients, rebuilt.reshape(1, ny, X)


def solution(mesh):
    return jax.shard_map(
        functools.partial(per_device, mesh.shape["ba"]),
        mesh=mesh,
        in_specs=(P("aa", None, "ba"), P()),
        out_specs=(P(None, "aa", "ba"), P("aa", None, "ba")),
        check_vma=False,
    )
```
